256 devices in a mesh: tile: 128 (over y, z_hi, x, core), lev: 2 (over z_lo).
Axes of the slice: x: 4, y: 4, z: 8 (z_hi: 4, z_lo: 2; z = z_hi * 2 + z_lo), core: 2. Of those that a mesh axis runs over, the one named last changes fastest.
Arguments:
- fields: float32 [4, 64, 2048, 128], P(None, 'lev', 'tile'), may hold values from -6 to 6
- horizontal_mix: float32 [64, 2048, 128], P('lev', 'tile'), may hold values from 0.1 to 0.2
- vertical_mix: float32 [64, 2048, 128], P('lev', 'tile'), may hold values from 0.03 to 0.07
- edge_flip: int32 [128], replicated, may hold values 0 or 1
- batch_slots: int32 [128, 128, 16], replicated, may hold values from -1 to 2047, as said below
- w_first: bfloat16 [4, 64, 768], replicated, may hold values from -1 to 1
- bias_first: float32 [768], replicated, may hold values from -3 to 3
- w_middle: bfloat16 [4, 768, 768], replicated, may hold values from -0.375 to 0.375
- bias_middle: float32 [4, 768], replicated, may hold values from -3 to 3
- w_output: bfloat16 [768, 4, 64], P(None, None, 'lev'), may hold values from -0.21875 to 0.21875
Outputs:
- advanced: float32 [4, 64, 2048, 128], P(None, 'lev', 'tile')
- tendency: bfloat16 [4, 64, 2048, 128], P(None, 'lev', 'tile')
The draws below stay inside these ranges and needn't reach their ends.
Inputs may be any that keep to these rules, and one draw needn't show every extreme that they name: Each tile's entries batch_slots[s] are either all -1 (an inactive tile) or hold each of its 2048 cell numbers exactly once; exactly 32 tiles are active. Entry [s, b, j] places a cell of tile s in slot j of physics batch b, so every batch receives exactly 16 columns from every active tile.
All inputs are finite; a program needn't handle non-finite values.
Results may differ from the reference program's by a relative error of at most 0.01.
Values may be sent and summed in bfloat16 or wider, within the bound.
No kernel may reach another device: no remote copies, remote signals or barrier semaphores. Data moves between devices by JAX's collectives and lax.ppermute only.
A program may use at most 64 MiB of HBM per device.

```python
import math
import jax
import jax.numpy as jnp
from jax import lax

CX = 16
CY = 128
LEV = 64
HID = 768
DEPTH = 4
SUB = 3
TILES = 128
NX = 2048
CELLS = 2048
CAP = 16


def draw_batch_slots(key, part):
    key = jax.random.fold_in(key, 7)
    key_tiles, key_cells = jax.random.split(key)
    order = jax.random.permutation(key_tiles, TILES)
    active = jnp.zeros((TILES,), jnp.int32).at[order[:TILES // 4]].set(1)
    keys = jax.random.split(key_cells, TILES)
    cells = jax.vmap(lambda single: jax.random.permutation(single, CELLS))(keys).astype(jnp.int32)
    cells = cells.reshape(TILES, TILES, CAP)
    return jnp.where(active[:, None, None] > 0, cells, -1).astype(jnp.int32)


def draw_fields(key, part):
    key = jax.random.fold_in(key, 11)
    key_sign, key_noise = jax.random.split(key)
    signs = (2 * jax.random.randint(key_sign, (4, LEV, NX, 1), 0, 2) - 1).astype(jnp.float32)
    noise = jax.random.normal(key_noise, (4, LEV, NX, CY), jnp.float32)
    values = 2.5 * signs + noise
    return jnp.clip(values, -6.0, 6.0).astype(jnp.float32)


def place_ends(array, stream_key, smallest, top_value):
    index_at = [jax.random.randint(jax.random.fold_in(stream_key, axis), (), 0, length) for axis, length in enumerate(array.shape)]
    main_axis = array.shape.index(max(array.shape))
    beside = index_at[:main_axis] + [(index_at[main_axis] + 1) % array.shape[main_axis]] + index_at[main_axis + 1:]
    return array.at[tuple(index_at)].set(smallest).at[tuple(beside)].set(top_value)


def steps_of(own_key, extent, cuts, low, top_value):
    def one(dim, blocks):
        steps = jax.random.uniform(jax.random.fold_in(jax.random.fold_in(own_key, 6), dim), (blocks,), jnp.float32, low / len(cuts), top_value / len(cuts))
        return jnp.repeat(jnp.exp(steps), extent[dim] // blocks).reshape((-1,) + (1,) * (len(extent) - dim - 1))

    factor_of = one(*cuts[0])
    for cut in cuts[1:]:
        factor_of = factor_of * one(*cut)
    return factor_of


def scatter_about(own_key, shape, deviation, reach, pieces=(), kind=jnp.bfloat16):
    entries = jax.random.normal(own_key, shape, jnp.float32) * deviation
    if len(pieces) > 0:
        entries = steps_of(own_key, shape, pieces, -0.22, 0.18) * entries
    return jnp.clip(entries, min=-reach, max=reach).astype(kind)


def setup_inputs(seed: int = 0) -> dict:
    key_of = jax.random.split(jax.random.key(seed), 11)
    fields = draw_fields(jax.random.fold_in(key_of[10], 71), 0)
    horizontal_mix = jnp.clip(jnp.exp(math.log(0.2) - 0.6931472 * jax.random.uniform(key_of[1], (LEV, NX, CY), jnp.float32) ** steps_of(key_of[1], (LEV, NX, CY), ((0, 2), (1, 128)), -0.2, 0.2)), 0.1, 0.2)
    vertical_mix = jnp.clip(jnp.exp(math.log(0.07) - 0.8472979 * jax.random.uniform(key_of[2], (LEV, NX, CY), jnp.float32) ** steps_of(key_of[2], (LEV, NX, CY), ((0, 2), (1, 128)), -0.2, 0.2)), 0.03, 0.07)
    edge_flip = place_ends((jax.random.randint(key_of[3], (TILES,), 0, 2) < 1).astype(jnp.int32), jax.random.fold_in(key_of[3], 1), 0, 1)
    batch_slots = draw_batch_slots(jax.random.fold_in(key_of[10], 71), 0)
    w_first = scatter_about(key_of[5], (4, LEV, HID), (4 * LEV // 6) ** -0.5, 1.0)
    bias_first = scatter_about(key_of[6], (HID,), 0.5, 3.0, (), jnp.float32)
    w_middle = scatter_about(key_of[7], (DEPTH, HID, HID), (HID // 3) ** -0.5, 0.375)
    bias_middle = scatter_about(key_of[8], (DEPTH, HID), 0.5, 3.0, (), jnp.float32)
    w_output = scatter_about(key_of[9], (HID, 4, LEV), HID ** -0.5, 0.21875, ((2, 2),))
    return {"fields": fields, "horizontal_mix": horizontal_mix, "vertical_mix": vertical_mix, "edge_flip": edge_flip, "batch_slots": batch_slots, "w_first": w_first, "bias_first": bias_first, "w_middle": w_middle, "bias_middle": bias_middle, "w_output": w_output}


def side_values(grid, edge_flip, shift):
    rolled = jnp.roll(grid, shift, axis=-2)
    column = jnp.arange(CX * TILES)
    if shift == 1:
        on_edge = column % CX == 0
        owner = column // CX
    else:
        on_edge = column % CX == CX - 1
        owner = (column // CX + 1) % TILES
    condition = (on_edge & (edge_flip[owner] > 0))[:, None]
    return jnp.where(condition, rolled[..., ::-1], rolled)


def level_above(grid, axis):
    edge = jnp.zeros_like(lax.slice_in_dim(grid, 0, 1, axis=axis))
    return jnp.concatenate([lax.slice_in_dim(grid, 1, grid.shape[axis], axis=axis), edge], axis=axis)


def level_below(grid, axis):
    edge = jnp.zeros_like(lax.slice_in_dim(grid, 0, 1, axis=axis))
    return jnp.concatenate([edge, lax.slice_in_dim(grid, 0, grid.shape[axis] - 1, axis=axis)], axis=axis)


def advance(fields, horizontal_mix, vertical_mix, edge_flip):
    mix_west = 0.5 * (horizontal_mix + side_values(horizontal_mix, edge_flip, 1))
    mix_east = 0.5 * (horizontal_mix + side_values(horizontal_mix, edge_flip, -1))
    mix_north = 0.5 * (horizontal_mix + jnp.roll(horizontal_mix, -1, axis=-1))
    mix_south = 0.5 * (horizontal_mix + jnp.roll(horizontal_mix, 1, axis=-1))
    mix_upper = 0.5 * (vertical_mix + level_above(vertical_mix, 0))
    mix_lower = 0.5 * (vertical_mix + level_below(vertical_mix, 0))
    for step in range(SUB):
        change = mix_west * (side_values(fields, edge_flip, 1) - fields)
        change = change + mix_east * (side_values(fields, edge_flip, -1) - fields)
        change = change + mix_north * (jnp.roll(fields, -1, axis=-1) - fields)
        change = change + mix_south * (jnp.roll(fields, 1, axis=-1) - fields)
        change = change + mix_upper * (level_above(fields, 1) - fields)
        change = change + mix_lower * (level_below(fields, 1) - fields)
        fields = fields + change
    return fields


def column_net(inputs, w_first, bias_first, w_middle, bias_middle, w_output):
    hidden = jnp.dot(inputs, w_first.reshape(-1, w_first.shape[2]), preferred_element_type=jnp.float32)
    hidden = jax.nn.silu(hidden + bias_first).astype(jnp.bfloat16)
    for layer in range(DEPTH):
        hidden = jnp.dot(hidden, w_middle[layer], preferred_element_type=jnp.float32)
        hidden = jax.nn.silu(hidden + bias_middle[layer]).astype(jnp.bfloat16)
    result = jnp.dot(hidden, w_output.reshape(w_output.shape[0], -1), preferred_element_type=jnp.float32)
    return result.astype(jnp.bfloat16)


def reference(fields, horizontal_mix, vertical_mix, edge_flip, batch_slots, w_first, bias_first, w_middle, bias_middle, w_output):
    advanced = advance(fields, horizontal_mix, vertical_mix, edge_flip)
    columns = advanced.astype(jnp.bfloat16).reshape(4, LEV, TILES, CX, CY)
    columns = columns.transpose(2, 3, 4, 0, 1).reshape(TILES * CELLS, 4 * LEV)
    tile_ids = jnp.arange(TILES, dtype=jnp.int32)[:, None, None]
    marks = jnp.where(batch_slots >= 0, tile_ids * CELLS + batch_slots, TILES * CELLS).reshape(-1).astype(jnp.int32)
    active = jnp.zeros((TILES * CELLS + 1,), jnp.int32).at[marks].set(1)[: TILES * CELLS]
    order = jnp.argsort(1 - active, stable=True)[: (TILES // 4) * CELLS].astype(jnp.int32)
    picked = columns[order].reshape(TILES // 4, CELLS, 4 * LEV)
    results = lax.map(lambda block: column_net(block, w_first, bias_first, w_middle, bias_middle, w_output), picked)
    results = results.reshape(-1, 4 * LEV)
    tendency = jnp.zeros((TILES * CELLS, 4 * LEV), jnp.bfloat16).at[order].set(results)
    tendency = tendency.reshape(TILES, CX, CY, 4, LEV).transpose(3, 4, 0, 1, 2).reshape(4, LEV, TILES * CX, CY)
    return advanced, tendency
```

```python
import jax
import jax.numpy as jnp
from jax import lax
from jax.experimental import pallas as pl
from jax.experimental.pallas import tpu as pltpu
from jax.sharding import PartitionSpec as P

CX, CY, HALF, NF = 16, 128, 32, 4
HID, DEPTH = 768, 4
FEAT = NF * HALF
PIECES = (2, 2, 2, 2)
ROWS = 24
OWN = 5
SLOTS = HALF + 10
BLOCK = 4
SIDE = (3 * NF + 3 + 2) * HALF
LEVS = (3 * NF + 2 + 3) * CX
DIAG = 32
VM = pl.BlockSpec(memory_space=pltpu.VMEM)
SM = pl.BlockSpec(memory_space=pltpu.SMEM)
HB = pl.BlockSpec(memory_space=pltpu.HBM)
F32, BF16 = jnp.float32, jnp.bfloat16
PARAMS = pltpu.CompilerParams(vmem_limit_bytes=24 * 1024 * 1024)


def shape(rows, dtype=BF16):
    return jax.ShapeDtypeStruct((rows, CY), dtype)


def side_channels():
    return [(c, d) for c in range(NF + 1) for d in range(3)] + [(NF + 1, 0), (NF + 1, 1)]


def lev_channels():
    return [(c, d) for c in range(NF) for d in range(3)] + [(NF, 0), (NF, 1)] + [(NF + 1, d) for d in range(3)]


DIAG_CELLS = [(0, 0), (1, 0), (0, 1)]


def pack_kernel(fields_hbm, hmix_hbm, vmix_hbm, far, near, up, d_far, d_near, fields, hmix, vmix, sems):
    lev = lax.axis_index("lev")
    odd = lax.axis_index("tile") % 2
    copies = [
        pltpu.make_async_copy(src, dst, sems.at[i])
        for i, (src, dst) in enumerate(((fields_hbm, fields), (hmix_hbm, hmix), (vmix_hbm, vmix)))
    ]
    for copy in copies:
        copy.start()
    for copy in copies:
        copy.wait()
    fields, hmix, vmix = fields.reshape(FEAT * CX, CY), hmix.reshape(HALF * CX, CY), vmix.reshape(HALF * CX, CY)

    def source(c):
        return (fields, c * HALF * CX) if c < NF else ((hmix, 0) if c == NF else (vmix, 0))

    def near_x(d):
        return jnp.where(odd == 0, CX - 1 - d, d)

    def far_x(d):
        return jnp.where(odd == 0, d, CX - 1 - d)

    for k, (c, d) in enumerate(side_channels()):
        ref, base = source(c)
        rows = pl.ds(k * HALF, HALF)
        far[rows, :] = ref[pl.ds(base + far_x(d), HALF, stride=CX), :].astype(BF16)
        near[rows, :] = ref[pl.ds(base + near_x(d), HALF, stride=CX), :].astype(BF16)
    for k, (c, d) in enumerate(lev_channels()):
        ref, base = source(c)
        at = jnp.where(lev == 0, HALF - 1 - d, d) * CX + base
        up[pl.ds(k * CX, CX), :] = ref[pl.ds(pl.multiple_of(at, CX), CX), :].astype(BF16)
    for out, place in ((d_far, far_x), (d_near, near_x)):
        cells = []
        for c in range(NF + 2):
            ref, base = source(c)
            for dx, dl in DIAG_CELLS:
                at = jnp.where(lev == 0, HALF - 1 - dl, dl) * CX + base
                cells.append(ref[pl.ds(at + place(dx), 1), :])
        cells.append(jnp.zeros((DIAG - len(cells), CY), F32))
        out[...] = jnp.concatenate(cells, axis=0).astype(BF16)


def dynamics_kernel(flags, fields_hbm, hmix_hbm, vmix_hbm, from_far, from_near, from_lev, d_far, d_near, *rest):
    count = len(PIECES)
    outs, scratch = rest[: 1 + 2 * count], rest[1 + 2 * count :]
    advanced, own, other = outs[0], outs[1 : 1 + count], outs[1 + count :]
    s0, s1, s2, hv, coef, sems = scratch
    lev = flags[2]
    odd = flags[4]
    copies = []
    for c in range(NF):
        copies.append((fields_hbm.at[c], s0.at[c, OWN : OWN + HALF, 0:CX]))
    copies.append((hmix_hbm, hv.at[0, OWN : OWN + HALF, 0:CX]))
    copies.append((vmix_hbm, hv.at[1, OWN : OWN + HALF, 0:CX]))
    copies = [pltpu.make_async_copy(src, dst, sems.at[i]) for i, (src, dst) in enumerate(copies)]
    for copy in copies:
        copy.start()

    s0 = s0.reshape(NF * SLOTS * ROWS, CY)
    hv = hv.reshape(2 * SLOTS * ROWS, CY)

    def place(c, slot):
        ref, k = (s0, c) if c < NF else (hv, c - NF)
        return ref, (k * SLOTS + slot) * ROWS

    zero = jnp.zeros((ROWS, CY), F32)
    ghost = jnp.where(lev == 0, OWN - 1, OWN + HALF)

    def still(ref):
        for f in range(NF):
            ref[pl.ds(pl.multiple_of((f * SLOTS + ghost) * ROWS, 8), ROWS), :] = zero

    still(s0)
    hv[pl.ds(pl.multiple_of((SLOTS + ghost) * ROWS, 8), ROWS), :] = zero

    row = lax.broadcasted_iota(jnp.int32, (CY, CY), 0)
    col = lax.broadcasted_iota(jnp.int32, (CY, CY), 1)

    def turned(flag, value):
        turn = jnp.where(jnp.where(flag > 0, CY - 1 - row, row) == col, 1.0, 0.0).astype(BF16)
        return jnp.dot(value, turn, preferred_element_type=F32)

    def near_row(d):
        return jnp.where(odd == 0, CX + d, ROWS - 1 - d)

    def far_row(d):
        return jnp.where(odd == 0, ROWS - 1 - d, CX + d)

    def beyond(d):
        return jnp.where(lev == 0, OWN + HALF + d, OWN - 1 - d)

    for flag, sides, corners, at_row in ((flags[0], from_near, d_near, near_row), (flags[1], from_far, d_far, far_row)):
        sides = turned(flag, sides[...])
        corners = turned(flag, corners[...])
        for k, (c, d) in enumerate(side_channels()):
            ref, base = place(c, OWN)
            ref[pl.ds(base + at_row(d), HALF, stride=ROWS), :] = sides[k * HALF : (k + 1) * HALF]
        for c in range(NF + 2):
            for n, (dx, dl) in enumerate(DIAG_CELLS):
                ref, base = place(c, beyond(dl))
                k = c * len(DIAG_CELLS) + n
                ref[pl.ds(base + at_row(dx), 1), :] = corners[k : k + 1]
    for k, (c, d) in enumerate(lev_channels()):
        ref, base = place(c, beyond(d))
        ref[pl.ds(pl.multiple_of(base, 8), CX), :] = from_lev[pl.ds(k * CX, CX), :].astype(F32)
    for copy in copies:
        copy.wait()

    def load(ref, k, slot, levels, rows=ROWS):
        at = pl.multiple_of((k * SLOTS + slot) * ROWS, 8)
        return ref[pl.ds(at, levels * ROWS), :].reshape(levels, ROWS, CY)[:, :rows]

    def save(ref, k, slot, value):
        levels = value.shape[0]
        at = pl.multiple_of((k * SLOTS + slot) * ROWS, 8)
        ref[pl.ds(at, levels * ROWS), :] = value.reshape(levels * ROWS, CY)

    def coefficients(at):
        h = 0.5 * load(hv, 0, at, BLOCK)
        v = 0.5 * load(hv, 1, at - 1, BLOCK + 2)
        pairs = v[1:] + v[:-1]
        upper, lower = pairs[1:], pairs[:-1]
        c_east = h + pltpu.roll(h, ROWS - 1, 1)
        c_west = h + pltpu.roll(h, 1, 1)
        c_north = h + pltpu.roll(h, CY - 1, 2)
        c_south = h + pltpu.roll(h, 1, 2)
        centre = 1.0 - (((c_east + c_west) + (c_north + c_south)) + (upper + lower))
        k = (c_east, c_west, c_north, c_south, upper, lower, centre)
        for n, value in enumerate(k):
            save(coef, n, at, value)
        return k

    def substep(source, k, at, rows, store):
        for f in range(NF):
            column = load(source, f, at - 1, BLOCK + 2)
            cell, centre = column[1:-1], column[1:-1, :rows]
            value = k[6] * centre
            value += k[0] * pltpu.roll(cell, ROWS - 1, 1)[:, :rows]
            value += k[1] * pltpu.roll(cell, 1, 1)[:, :rows]
            value += k[2] * pltpu.roll(centre, CY - 1, 2)
            value += k[3] * pltpu.roll(centre, 1, 2)
            value += k[4] * column[2:, :rows]
            value += k[5] * column[:-2, :rows]
            store(f, at, value)

    def kept(at, rows):
        return [load(coef, n, at, BLOCK, rows) for n in range(7)]

    def into(target):
        return lambda f, at, value: save(target, f, at, value)

    def final(f, at, value):
        advanced[pl.ds(pl.multiple_of((f * HALF + at - OWN) * CX, CX), BLOCK * CX), :] = value.reshape(BLOCK * CX, CY)

    def one(i):
        at = OWN - 2 + i * BLOCK
        substep(s0, coefficients(at), at, ROWS, into(s1))

    def two(i):
        at = OWN - 3 + (i - 1) * BLOCK
        substep(s1, kept(at, ROWS), at, ROWS, into(s2))

    def three(i):
        at = OWN + (i - 3) * BLOCK
        substep(s2, kept(at, CX), at, CX, final)

    def sweep(i, parts):
        for part in parts:
            part(i)
        still(s1)
        still(s2)

    last = HALF // BLOCK
    sweep(0, (one,))
    for i in (1, 2):
        sweep(i, (two, one))

    for i in range(3, last + 1):
        sweep(i, (three, two, one))
    sweep(last + 1, (three, two))
    sweep(last + 2, (three,))

    x = 0
    for piece, width in enumerate(PIECES):
        for i in range(width):
            low = advanced[pl.ds(x, FEAT, stride=CX), :].astype(BF16)
            high = advanced[pl.ds(x + CX // 2, FEAT, stride=CX), :].astype(BF16)
            rows = pl.ds(i * FEAT, FEAT)
            own[piece][rows, :] = jnp.where(lev == 0, low, high)
            other[piece][rows, :] = jnp.where(lev == 0, high, low)
            x += 1


def prepare_kernel(
    early, edge_flip, batch_slots, w_first, w_mid, b_first, b_mid,
    flags, w_first_out, w_mid_out, b_first_out, b_mid_out, flips, slots, sems,
):
    place = lax.axis_index("tile")
    odd = place % 2
    count = edge_flip.shape[0]
    pairs = (
        (edge_flip, flips),
        (batch_slots.at[place, 0:8], slots),
        (w_mid, w_mid_out),
        (w_first, w_first_out),
    )
    copies = [pltpu.make_async_copy(src, dst, sems.at[i]) for i, (src, dst) in enumerate(pairs)]
    for copy in copies:
        copy.start()
    b_first_out[...] = jnp.broadcast_to(b_first[...], (CY, HID)).T
    for k in range(DEPTH):
        b_mid_out[pl.ds(k * HID, HID), :] = jnp.broadcast_to(b_mid[k : k + 1, :], (CY, HID)).T
    for copy in copies:
        copy.wait()
    east = flips[(place + 1) % count]
    west = flips[place]
    flags[0] = jnp.where(odd == 0, east, west)
    flags[1] = jnp.where(odd == 0, west, east)
    flags[2] = lax.axis_index("lev")
    flags[3] = jnp.where(slots[0, 0] >= 0, 1, 0)
    flags[4] = odd


def silu(z):
    half = 0.5 * z
    return half + half * jnp.tanh(half)


def net_kernel(flags, own, other, w_first, b_first, w_mid, b_mid, wo_own, wo_other, out_own, out_other, ha, hb):
    n = own.shape[0] // FEAT
    lev = flags[2]
    tile = 256

    @pl.when(flags[3] > 0)
    def _():
        def flat(ref):
            return jnp.concatenate([ref[pl.ds(i * FEAT, FEAT), :] for i in range(n)], axis=1)

        def first_rows(block):
            return [w_first[pl.ds(pl.multiple_of(f * 2 * HALF + block * HALF, HALF), HALF), :] for f in range(NF)]

        def layer(weights, bias, start, value, target):
            for m in range(0, HID, tile):
                part = lax.dot_general(weights(m), value, (((0,), (0,)), ((), ())), preferred_element_type=F32)
                shift = bias[pl.ds(start + m, tile), :]
                target[pl.ds(m, tile), :] = silu(part + jnp.concatenate([shift] * n, axis=1)).astype(BF16)

        w0 = jnp.concatenate(first_rows(lev) + first_rows(1 - lev), axis=0)
        layer(lambda m: w0[:, m : m + tile], b_first, 0, jnp.concatenate([flat(own), flat(other)], axis=0), ha)
        source, target = ha, hb
        for k in range(DEPTH):
            layer(lambda m: w_mid[pl.ds(k * HID, HID), m : m + tile], b_mid, k * HID, source[...], target)
            source, target = target, source
        hidden = source[...]
        for w, out in ((wo_other, out_other), (wo_own, out_own)):
            result = jnp.dot(w[...], hidden, preferred_element_type=F32).astype(BF16)
            for i in range(n):
                out[pl.ds(i * FEAT, FEAT), :] = result[:, i * CY : (i + 1) * CY]


def finish_kernel(flags, *rest):
    count = len(PIECES)
    mine, theirs = rest[:count], rest[count : 2 * count]
    tendency, wide = rest[2 * count :]
    lev = flags[2]
    active = flags[3] > 0

    @pl.when(active)
    def _():
        x = 0
        for piece, width in enumerate(PIECES):
            for i in range(width):
                rows = pl.ds(i * FEAT, FEAT)
                a, b = mine[piece][rows, :], theirs[piece][rows, :]
                wide[pl.ds(x, FEAT, stride=CX), :] = jnp.where(lev == 0, a, b).astype(F32)
                wide[pl.ds(x + CX // 2, FEAT, stride=CX), :] = jnp.where(lev == 0, b, a).astype(F32)
                x += 1
        tendency[...] = wide[...].astype(BF16)

    @pl.when(jnp.logical_not(active))
    def _():
        tendency[...] = jnp.zeros(tendency.shape, BF16)


def along_lev(value):
    return lax.ppermute(value, "lev", [(0, 1), (1, 0)])


def across(value, first, turn):
    count = lax.axis_size("tile")
    pairs = []
    for i in range(first, count, 2):
        for k in range(2):
            a, b = 2 * i + k, 2 * ((i + 1) % count) + (1 - k if turn else k)
            pairs += [(a, b), (b, a)]
    return lax.ppermute(value, ("tile", "lev"), sorted(pairs))


def on_device(
    fields, horizontal_mix, vertical_mix, edge_flip, batch_slots,
    w_first, bias_first, w_middle, bias_middle, w_output,
):
    fields_hbm, hmix_hbm, vmix_hbm = (
        pltpu.with_memory_space_constraint(value, pltpu.HBM) for value in (fields, horizontal_mix, vertical_mix)
    )
    far, near, up, d_far, d_near = pl.pallas_call(
        pack_kernel,
        in_specs=[HB] * 3,
        out_specs=[VM] * 5,
        out_shape=[shape(SIDE), shape(SIDE), shape(LEVS), shape(DIAG), shape(DIAG)],
        scratch_shapes=[
            pltpu.VMEM((NF, HALF, CX, CY), F32),
            pltpu.VMEM((HALF, CX, CY), F32),
            pltpu.VMEM((HALF, CX, CY), F32),
            pltpu.SemaphoreType.DMA((3,)),
        ],
        compiler_params=PARAMS,
    )(fields_hbm, hmix_hbm, vmix_hbm)
    from_far = across(far, 1, False)
    from_lev = along_lev(up)
    from_near = across(near, 0, False)
    from_d_near = across(d_near, 0, True)
    from_d_far = across(d_far, 1, True)

    def in_hbm(value):
        return pltpu.with_memory_space_constraint(value, pltpu.HBM)

    flags, w_first_v, w_mid_v, b_first, b_mid = pl.pallas_call(
        prepare_kernel,
        in_specs=[HB] * 5 + [VM, VM],
        out_specs=[SM] + [VM] * 4,
        out_shape=[
            jax.ShapeDtypeStruct((5,), jnp.int32),
            pltpu.VMEM((2 * FEAT, HID), BF16),
            pltpu.VMEM((DEPTH * HID, HID), BF16),
            pltpu.VMEM((HID, CY), F32),
            pltpu.VMEM((DEPTH * HID, CY), F32),
        ],
        scratch_shapes=[
            pltpu.SMEM(edge_flip.shape, jnp.int32),
            pltpu.SMEM((8, batch_slots.shape[1]), jnp.int32),
            pltpu.SemaphoreType.DMA((4,)),
        ],
        compiler_params=PARAMS,
    )(
        in_hbm(d_near),
        in_hbm(edge_flip),
        in_hbm(batch_slots.transpose(0, 2, 1)),
        in_hbm(w_first.reshape(2 * FEAT, HID)),
        in_hbm(w_middle.reshape(DEPTH * HID, HID)),
        bias_first.reshape(1, HID),
        bias_middle,
    )
    wo_own = w_output.reshape(HID, FEAT).T
    flags, wo_own, from_far, from_lev, from_near, from_d_near, from_d_far = lax.optimization_barrier(
        (flags, wo_own, from_far, from_lev, from_near, from_d_near, from_d_far)
    )
    wo_other = along_lev(wo_own)

    outs = pl.pallas_call(
        dynamics_kernel,
        in_specs=[SM] + [HB] * 3 + [VM] * 5,
        out_specs=[VM] * (1 + 2 * len(PIECES)),
        out_shape=[shape(FEAT * CX, F32)] + [shape(n * FEAT) for n in PIECES] * 2,
        scratch_shapes=[
            pltpu.VMEM((NF, SLOTS, ROWS, CY), F32),
            pltpu.VMEM((NF * SLOTS * ROWS, CY), F32),
            pltpu.VMEM((NF * SLOTS * ROWS, CY), F32),
            pltpu.VMEM((2, SLOTS, ROWS, CY), F32),
            pltpu.VMEM((7 * SLOTS * ROWS, CY), F32),
            pltpu.SemaphoreType.DMA((NF + 2,)),
        ],
        compiler_params=PARAMS,
    )(flags, fields_hbm, hmix_hbm, vmix_hbm, from_far, from_near, from_lev, from_d_far, from_d_near)
    advanced, own, other = outs[0], outs[1 : 1 + len(PIECES)], outs[1 + len(PIECES) :]

    received = [along_lev(piece) for piece in other]
    mine, theirs = [], []
    for k, width in enumerate(PIECES):
        rows = width * FEAT
        a, b = pl.pallas_call(
            net_kernel,
            in_specs=[SM] + [VM] * 8,
            out_specs=[VM] * 2,
            out_shape=[shape(rows)] * 2,
            scratch_shapes=[pltpu.VMEM((HID, width * CY), BF16)] * 2,
            compiler_params=PARAMS,
        )(
            flags, own[k], received[k], w_first_v, b_first, w_mid_v, b_mid, wo_own, wo_other
        )
        mine.append(a)
        theirs.append(along_lev(b))
    tendency = pl.pallas_call(
        finish_kernel,
        in_specs=[SM] + [VM] * (2 * len(PIECES)),
        out_specs=VM,
        out_shape=shape(FEAT * CX),
        scratch_shapes=[pltpu.VMEM((FEAT * CX, CY), F32)],
        compiler_params=PARAMS,
    )(flags, *mine, *theirs)
    whole = (NF, HALF, CX, CY)
    return advanced.reshape(whole), tendency.reshape(whole)


def solution(mesh):
    return jax.shard_map(
        on_device,
        mesh=mesh,
        in_specs=(
            P(None, "lev", "tile", None),
            P("lev", "tile", None),
            P("lev", "tile", None),
            P(),
            P(),
            P(),
            P(),
            P(),
            P(),
            P(None, None, "lev"),
        ),
        out_specs=(P(None, "lev", "tile", None), P(None, "lev", "tile", None)),
        check_vma=False,
    )
```

```python
import jax
import jax.numpy as jnp
from jax import lax
from jax.experimental import pallas as pl
from jax.experimental.pallas import tpu as pltpu
from jax.sharding import PartitionSpec as P

CX, CY, HALF, NF = 16, 128, 32, 4
HID, DEPTH = 768, 4
FEAT = NF * HALF
PIECES = (5,)
SPLIT = sum(PIECES)
SHARED = CX - 2 * SPLIT
ROWS = 24
OWN = 5
SLOTS = HALF + 10
BLOCK = 4
SIDE = (3 * NF + 3 + 2) * HALF
LEVS = (3 * NF + 2 + 3) * CX
LEV_SIDES = 8 * (3 * NF + 2 + 3 + 1)
VM = pl.BlockSpec(memory_space=pltpu.VMEM)
SM = pl.BlockSpec(memory_space=pltpu.SMEM)
HB = pl.BlockSpec(memory_space=pltpu.HBM)
F32, BF16 = jnp.float32, jnp.bfloat16
PARAMS = pltpu.CompilerParams(vmem_limit_bytes=24 * 1024 * 1024)


def cost(us):
    return pl.CostEstimate(flops=0, transcendentals=0, bytes_accessed=int(us * 3_600_000))


def shape(rows, dtype=BF16):
    return jax.ShapeDtypeStruct((rows, CY), dtype)


def side_channels():
    return [(c, d) for c in range(NF + 1) for d in range(3)] + [(NF + 1, 0), (NF + 1, 1)]


def lev_channels():
    return [(c, d) for c in range(NF) for d in range(3)] + [(NF, 0), (NF, 1)] + [(NF + 1, d) for d in range(3)]


def near_row(odd, d):
    return jnp.where(odd == 0, CX + d, ROWS - 1 - d)


def far_row(odd, d):
    return jnp.where(odd == 0, ROWS - 1 - d, CX + d)


def views(s0, hv):
    return s0.reshape(NF * SLOTS * ROWS, CY), hv.reshape(2 * SLOTS * ROWS, CY)


def place_in(s0, hv, c, slot):
    ref, k = (s0, c) if c < NF else (hv, c - NF)
    return ref, (k * SLOTS + slot) * ROWS


def beyond(lev, d):
    return jnp.where(lev == 0, OWN + HALF + d, OWN - 1 - d)


def pack_kernel(fields, hmix, vmix, which, s0, hv, far, near, sems):
    odd = lax.axis_index("tile") % 2
    which[0] = lax.axis_index("lev")
    which[1] = odd
    pairs = [(fields.at[c], s0.at[c, OWN : OWN + HALF, 0:CX]) for c in range(NF)]
    pairs += [(hmix, hv.at[0, OWN : OWN + HALF, 0:CX]), (vmix, hv.at[1, OWN : OWN + HALF, 0:CX])]
    copies = [pltpu.make_async_copy(src, dst, sems.at[i]) for i, (src, dst) in enumerate(pairs)]
    for copy in copies:
        copy.start()
    for copy in copies:
        copy.wait()
    s0, hv = views(s0, hv)
    for k, (c, d) in enumerate(side_channels()):
        ref, base = place_in(s0, hv, c, OWN)
        rows = pl.ds(k * HALF, HALF)
        far_x = jnp.where(odd == 0, d, CX - 1 - d)
        near_x = CX - 1 - far_x
        far[rows, :] = ref[pl.ds(base + far_x, HALF, stride=ROWS), :].astype(BF16)
        near[rows, :] = ref[pl.ds(base + near_x, HALF, stride=ROWS), :].astype(BF16)


def flags_kernel(which, edge_flip, batch_slots, flags, flips, slots, sems):
    tile = lax.axis_index("tile")
    pairs = ((edge_flip, flips), (batch_slots.at[tile, 0:8], slots))
    copies = [pltpu.make_async_copy(src, dst, sems.at[i]) for i, (src, dst) in enumerate(pairs)]
    for copy in copies:
        copy.start()
    for copy in copies:
        copy.wait()
    odd = which[1]
    east = flips[(tile + 1) % edge_flip.shape[0]]
    west = flips[tile]
    flags[0] = jnp.where(odd == 0, east, west)
    flags[1] = jnp.where(odd == 0, west, east)
    flags[2] = which[0]
    flags[3] = jnp.where(slots[0, 0] >= 0, 1, 0)
    flags[4] = odd


def still(ref, ghost, count):
    for f in range(count):
        ref[pl.ds(pl.multiple_of((f * SLOTS + ghost) * ROWS, 8), ROWS), :] = jnp.zeros((ROWS, CY), F32)


def edge_kernel(flags, s0_in, hv_in, from_near, from_far, s0, hv, up):
    lev, odd = flags[2], flags[4]
    s0, hv = views(s0, hv)
    ghost = jnp.where(lev == 0, OWN - 1, OWN + HALF)
    still(s0, ghost, NF)
    still(hv, ghost, 2)
    row = lax.broadcasted_iota(jnp.int32, (CY, CY), 0)
    col = lax.broadcasted_iota(jnp.int32, (CY, CY), 1)
    for flag, sides, at_row in ((flags[0], from_near, near_row), (flags[1], from_far, far_row)):
        turn = jnp.where(jnp.where(flag > 0, CY - 1 - row, row) == col, 1.0, 0.0).astype(BF16)
        columns = jnp.dot(sides[...], turn, preferred_element_type=F32)
        for k, (c, d) in enumerate(side_channels()):
            ref, base = place_in(s0, hv, c, OWN)
            ref[pl.ds(base + at_row(odd, d), HALF, stride=ROWS), :] = columns[k * HALF : (k + 1) * HALF]
    beside = []
    for k, (c, d) in enumerate(lev_channels()):
        slot = jnp.where(lev == 0, OWN + HALF - 1 - d, OWN + d)
        ref, base = place_in(s0, hv, c, slot)
        level = ref[pl.ds(pl.multiple_of(base, 8), ROWS), :]
        up[pl.ds(k * CX, CX), :] = level[:CX].astype(BF16)
        beside.append(level[CX:])
    beside.append(jnp.zeros((8, CY), F32))
    up[pl.ds(LEVS, LEV_SIDES), :] = jnp.concatenate(beside, axis=0).astype(BF16)


def load(ref, k, slot, levels, rows=ROWS):
    at = (k * SLOTS + slot) * ROWS
    at = at if isinstance(at, int) else pl.multiple_of(at, 8)
    return ref[pl.ds(at, levels * ROWS), :].reshape(levels, ROWS, CY)[:, :rows]


def save(ref, k, slot, value):
    at = (k * SLOTS + slot) * ROWS
    at = at if isinstance(at, int) else pl.multiple_of(at, 8)
    levels = value.shape[0]
    ref[pl.ds(at, levels * ROWS), :] = value.reshape(levels * ROWS, CY)


def coefficients(hv, coef, at, levels):
    h = 0.5 * load(hv, 0, at, levels)
    v = 0.5 * load(hv, 1, at - 1, levels + 2)
    pairs = v[1:] + v[:-1]
    upper, lower = pairs[1:], pairs[:-1]
    c_east = h + pltpu.roll(h, ROWS - 1, 1)
    c_west = h + pltpu.roll(h, 1, 1)
    c_north = h + pltpu.roll(h, CY - 1, 2)
    c_south = h + pltpu.roll(h, 1, 2)
    centre = 1.0 - (((c_east + c_west) + (c_north + c_south)) + (upper + lower))
    k = (c_east, c_west, c_north, c_south, upper, lower, centre)
    for n, value in enumerate(k):
        save(coef, n, at, value)
    return k


def kept(coef, at, levels, rows):
    return [load(coef, n, at, levels, rows) for n in range(7)]


def substep(source, k, at, levels, rows, store):
    for f in range(NF):
        column = load(source, f, at - 1, levels + 2)
        cell, centre = column[1:-1], column[1:-1, :rows]
        value = k[6] * centre
        value += k[0] * pltpu.roll(cell, ROWS - 1, 1)[:, :rows]
        value += k[1] * pltpu.roll(cell, 1, 1)[:, :rows]
        value += k[2] * pltpu.roll(centre, CY - 1, 2)
        value += k[3] * pltpu.roll(centre, 1, 2)
        value += k[4] * column[2:, :rows]
        value += k[5] * column[:-2, :rows]
        store(f, at, value)


def into(target):
    return lambda f, at, value: save(target, f, at, value)


def into_result(advanced):
    def store(f, at, value):
        start = (f * HALF + at - OWN) * CX
        start = start if isinstance(start, int) else pl.multiple_of(start, CX)
        advanced[pl.ds(start, value.shape[0] * CX), :] = value.reshape(value.shape[0] * CX, CY)

    return store


def dynamics_kernel(flags, s0, hv, w_first_hbm, w_mid_hbm, s1, s2, coef, advanced, w_first, w_mid, sems):
    copies = [
        pltpu.make_async_copy(src, dst, sems.at[i])
        for i, (src, dst) in enumerate(((w_first_hbm, w_first), (w_mid_hbm, w_mid)))
    ]
    for copy in copies:
        copy.start()
    s0, hv = views(s0, hv)
    lev = flags[2]
    ghost = jnp.where(lev == 0, OWN - 1, OWN + HALF)
    final = into_result(advanced)

    def one(i):
        at = OWN + i * BLOCK
        substep(s0, coefficients(hv, coef, at, BLOCK), at, BLOCK, ROWS, into(s1))

    def two(i):
        at = OWN - 1 + (i - 1) * BLOCK
        substep(s1, kept(coef, at, BLOCK, ROWS), at, BLOCK, ROWS, into(s2))

    def three(i):
        at = OWN + (i - 3) * BLOCK
        substep(s2, kept(coef, at, BLOCK, CX), at, BLOCK, CX, final)

    still(s1, ghost, NF)
    last = HALF // BLOCK
    for i in range(last + 3):
        if i >= 3:
            three(i)
        if 1 <= i <= last + 1:
            two(i)
        if i < last:
            one(i)
        if i in (1, last + 1):
            still(s2, ghost, NF)
    for copy in copies:
        copy.wait()


def closing_kernel(flags, s0_in, hv_in, s1_in, s2_in, coef_in, advanced_in, from_lev, s0, hv, s1, s2, coef, advanced, own, other):
    lev = flags[2]
    s0, hv = views(s0, hv)
    for k, (c, d) in enumerate(lev_channels()):
        ref, base = place_in(s0, hv, c, beyond(lev, d))
        base = pl.multiple_of(base, 8)
        ref[pl.ds(base, CX), :] = from_lev[pl.ds(k * CX, CX), :].astype(F32)
    sides = from_lev[pl.ds(LEVS, LEV_SIDES), :].astype(F32)
    for k, (c, d) in enumerate(lev_channels()):
        ref, base = place_in(s0, hv, c, beyond(lev, d))
        ref[pl.ds(pl.multiple_of(base + CX, 8), 8), :] = sides[k * 8 : (k + 1) * 8]
    at = jnp.where(lev == 0, OWN + HALF - 1, OWN - 2)
    substep(s0, coefficients(hv, coef, at, 3), at, 3, ROWS, into(s1))
    at = jnp.where(lev == 0, OWN + HALF - 2, OWN - 1)
    substep(s1, kept(coef, at, 3, ROWS), at, 3, ROWS, into(s2))
    at = jnp.where(lev == 0, OWN + HALF - 3, OWN)
    substep(s2, kept(coef, at, 3, CX), at, 3, CX, into_result(advanced))
    take_piece(lev, advanced, own, other, 0)


def take_columns(advanced, first, width, target):
    for i in range(width):
        target[pl.ds(i * FEAT, FEAT), :] = advanced[pl.ds(first + i, FEAT, stride=CX), :].astype(BF16)


def piece_start(lev, k):
    return jnp.where(lev == 0, 0, SPLIT) + sum(PIECES[:k])


def take_piece(lev, advanced, own, other, k):
    take_columns(advanced, piece_start(lev, k), PIECES[k], own)
    take_columns(advanced, piece_start(1 - lev, k), PIECES[k], other)


def rest_kernel(flags, advanced, shared, *pieces):
    lev = flags[2]
    for k in range(1, len(PIECES)):
        take_piece(lev, advanced, pieces[2 * k - 2], pieces[2 * k - 1], k)
    take_columns(advanced, 2 * SPLIT, SHARED, shared)


def silu(z):
    half = 0.5 * z
    return half + half * jnp.tanh(half)


def network(flags, own, other, w_first, b_first, w_mid, b_mid, ha, hb):
    n = own.shape[0] // FEAT
    lev = flags[2]

    def flat(ref):
        return jnp.concatenate([ref[pl.ds(i * FEAT, FEAT), :] for i in range(n)], axis=1)

    def first_rows(block):
        return [w_first[pl.ds(pl.multiple_of(f * 2 * HALF + block * HALF, HALF), HALF), :] for f in range(NF)]

    weights = jnp.concatenate(first_rows(lev) + first_rows(1 - lev), axis=0)
    inputs = jnp.concatenate([flat(own), flat(other)], axis=0)
    part = lax.dot_general(inputs, weights, (((0,), (0,)), ((), ())), preferred_element_type=F32)
    ha[...] = silu(part + b_first[...]).astype(BF16)
    source, target = ha, hb
    for k in range(DEPTH):
        part = jnp.dot(source[...], w_mid[pl.ds(k * HID, HID), :], preferred_element_type=F32)
        target[...] = silu(part + b_mid[k : k + 1, :]).astype(BF16)
        source, target = target, source
    return source[...]


def outputs(w, hidden):
    return lax.dot_general(w[...], hidden, (((1,), (1,)), ((), ())), preferred_element_type=F32)


def net_kernel(flags, own, other, w_first, b_first, w_mid, b_mid, wo_own, wo_other, out_own, out_other, ha, hb):
    @pl.when(flags[3] > 0)
    def _():
        hidden = network(flags, own, other, w_first, b_first, w_mid, b_mid, ha, hb)
        for w, out in ((wo_other, out_other), (wo_own, out_own)):
            result = outputs(w, hidden).astype(BF16)
            for i in range(own.shape[0] // FEAT):
                out[pl.ds(i * FEAT, FEAT), :] = result[:, i * CY : (i + 1) * CY]


def first_net_kernel(flags, advanced, *rest):
    target, sem = rest[10], rest[13]
    copy = pltpu.make_async_copy(advanced, target, sem)
    copy.start()
    net_kernel(flags, *rest[:10], *rest[11:13])
    copy.wait()


def put_columns(wide, first, source):
    for i in range(source.shape[0] // FEAT):
        wide[pl.ds(first + i, FEAT, stride=CX), :] = source[pl.ds(i * FEAT, FEAT), :].astype(F32)


def last_net_kernel(flags, own, other, w_first, b_first, w_mid, b_mid, wo_own, *rest):
    mine = rest[: len(PIECES)]
    wide, ha, hb = rest[len(PIECES) :]
    lev = flags[2]

    @pl.when(flags[3] > 0)
    def _():
        for k, source in enumerate(mine):
            put_columns(wide, piece_start(lev, k), source)
        result = outputs(wo_own, network(flags, own, other, w_first, b_first, w_mid, b_mid, ha, hb))
        for i in range(SHARED):
            wide[pl.ds(2 * SPLIT + i, FEAT, stride=CX), :] = result[:, i * CY : (i + 1) * CY]


def finish_kernel(flags, wide_in, *rest):
    theirs, wide, tendency = rest[:-2], rest[-2], rest[-1]
    lev = flags[2]
    active = flags[3] > 0

    @pl.when(active)
    def _():
        for k, source in enumerate(theirs):
            put_columns(wide, piece_start(1 - lev, k), source)
        tendency[...] = wide[...].astype(BF16)

    @pl.when(jnp.logical_not(active))
    def _():
        tendency[...] = jnp.zeros(tendency.shape, BF16)


def along_lev(value):
    return lax.ppermute(value, "lev", [(0, 1), (1, 0)])


def across(value, first):
    count = lax.axis_size("tile")
    pairs = [(i, (i + 1) % count) for i in range(first, count, 2)]
    return lax.ppermute(value, "tile", sorted(pairs + [(b, a) for a, b in pairs]))


def in_hbm(value):
    return pltpu.with_memory_space_constraint(value, pltpu.HBM)


def on_device(
    fields, horizontal_mix, vertical_mix, edge_flip, batch_slots,
    w_first, bias_first, w_middle, bias_middle, w_output,
):
    def scratch(*lead):
        return pltpu.VMEM((*lead, SLOTS, ROWS, CY), F32)

    def flat(count):
        return pltpu.VMEM((count * SLOTS * ROWS, CY), F32)

    which, s0, hv, far, near = pl.pallas_call(
        pack_kernel,
        in_specs=[HB] * 3,
        out_specs=[SM] + [VM] * 4,
        out_shape=[jax.ShapeDtypeStruct((2,), jnp.int32), scratch(NF), scratch(2), shape(SIDE), shape(SIDE)],
        scratch_shapes=[pltpu.SemaphoreType.DMA((NF + 2,))],
        cost_estimate=cost(2.1),
        compiler_params=PARAMS,
    )(in_hbm(fields), in_hbm(horizontal_mix), in_hbm(vertical_mix))
    from_far = across(far, 1)
    from_near = across(near, 0)
    flags = pl.pallas_call(
        flags_kernel,
        in_specs=[SM, HB, HB],
        out_specs=SM,
        out_shape=jax.ShapeDtypeStruct((5,), jnp.int32),
        scratch_shapes=[
            pltpu.SMEM(edge_flip.shape, jnp.int32),
            pltpu.SMEM((8, batch_slots.shape[1]), jnp.int32),
            pltpu.SemaphoreType.DMA((2,)),
        ],
        cost_estimate=cost(1.9),
        compiler_params=PARAMS,
    )(which, in_hbm(edge_flip), in_hbm(batch_slots.transpose(0, 2, 1)))
    s0, hv, up = pl.pallas_call(
        edge_kernel,
        in_specs=[SM] + [VM] * 4,
        out_specs=[VM] * 3,
        out_shape=[scratch(NF), scratch(2), shape(LEVS + LEV_SIDES)],
        input_output_aliases={1: 0, 2: 1},
        cost_estimate=cost(0.8),
        compiler_params=PARAMS,
    )(flags, s0, hv, from_near, from_far)
    from_lev = along_lev(up)
    wo_own, s0 = lax.optimization_barrier((w_output.reshape(HID, FEAT).T, s0))
    wo_other = along_lev(wo_own)
    s1, s2, coef, advanced, w_first_v, w_mid_v = pl.pallas_call(
        dynamics_kernel,
        in_specs=[SM, VM, VM, HB, HB],
        out_specs=[VM] * 6,
        out_shape=[
            flat(NF), flat(NF), flat(7), pltpu.VMEM((FEAT * CX, CY), F32),
            pltpu.VMEM((2 * FEAT, HID), BF16), pltpu.VMEM((DEPTH * HID, HID), BF16),
        ],
        scratch_shapes=[pltpu.SemaphoreType.DMA((2,))],
        cost_estimate=cost(5.8),
        compiler_params=PARAMS,
    )(flags, s0, hv, in_hbm(w_first.reshape(2 * FEAT, HID)), in_hbm(w_middle.reshape(DEPTH * HID, HID)))
    outs = pl.pallas_call(
        closing_kernel,
        in_specs=[SM] + [VM] * 7,
        out_specs=[VM] * 8,
        out_shape=[scratch(NF), scratch(2), flat(NF), flat(NF), flat(7), pltpu.VMEM((FEAT * CX, CY), F32)]
        + [shape(PIECES[0] * FEAT)] * 2,
        input_output_aliases={i + 1: i for i in range(6)},
        cost_estimate=cost(1.1),
        compiler_params=PARAMS,
    )(flags, s0, hv, s1, s2, coef, advanced, from_lev)
    advanced, own, other = outs[5:]
    sizes = [n for n in PIECES[1:] for _ in range(2)]
    shared, *pieces = pl.pallas_call(
        rest_kernel,
        in_specs=[SM, VM],
        out_specs=[VM] * (1 + len(sizes)),
        out_shape=[shape(n * FEAT) for n in [SHARED, *sizes]],
        cost_estimate=cost(0.8),
        compiler_params=PARAMS,
    )(flags, advanced)
    own, other = [own, *pieces[::2]], [other, *pieces[1::2]]
    received = [along_lev(piece) for piece in other]
    shared_other = along_lev(shared)

    b_first = bias_first.reshape(1, HID)
    mine, theirs = [], []
    for k, width in enumerate(PIECES):
        rows = width * FEAT
        a, b, *sent = pl.pallas_call(
            net_kernel if k > 0 else first_net_kernel,
            in_specs=[SM] + [VM] * (8 if k > 0 else 9),
            out_specs=[VM] * 2 + ([] if k > 0 else [HB]),
            out_shape=[shape(rows)] * 2 + ([] if k > 0 else [pltpu.HBM((FEAT * CX, CY), F32)]),
            scratch_shapes=[pltpu.VMEM((width * CY, HID), BF16)] * 2 + ([] if k > 0 else [pltpu.SemaphoreType.DMA]),
            cost_estimate=cost(0.4 + 1.05 * width),
            compiler_params=PARAMS,
        )(
            flags, *([] if k > 0 else [advanced]), own[k], received[k],
            w_first_v, b_first, w_mid_v, bias_middle, wo_own, wo_other,
        )
        if k == 0:
            result = sent[0]
        mine.append(a)
        theirs.append(along_lev(b))
    wide = pl.pallas_call(
        last_net_kernel,
        in_specs=[SM] + [VM] * (7 + len(PIECES)),
        out_specs=VM,
        out_shape=pltpu.VMEM((FEAT * CX, CY), F32),
        scratch_shapes=[pltpu.VMEM((SHARED * CY, HID), BF16)] * 2,
        cost_estimate=cost(4.3),
        compiler_params=PARAMS,
    )(flags, shared, shared_other, w_first_v, b_first, w_mid_v, bias_middle, wo_own, *mine)
    _, tendency = pl.pallas_call(
        finish_kernel,
        in_specs=[SM, VM] + [VM] * len(PIECES),
        out_specs=[VM, VM],
        out_shape=[pltpu.VMEM((FEAT * CX, CY), F32), shape(FEAT * CX)],
        input_output_aliases={1: 0},
        cost_estimate=cost(1.4),
        compiler_params=PARAMS,
    )(flags, wide, *theirs)
    whole = (NF, HALF, CX, CY)
    return result.reshape(whole), tendency.reshape(whole)


def solution(mesh):
    return jax.shard_map(
        on_device,
        mesh=mesh,
        in_specs=(
            P(None, "lev", "tile", None),
            P("lev", "tile", None),
            P("lev", "tile", None),
            P(),
            P(),
            P(),
            P(),
            P(),
            P(),
            P(None, None, "lev"),
        ),
        out_specs=(P(None, "lev", "tile", None), P(None, "lev", "tile", None)),
        check_vma=False,
    )
```

```python
import jax
import jax.numpy as jnp
from jax import lax
from jax.experimental import pallas as pl
from jax.experimental.pallas import tpu as pltpu
from jax.sharding import PartitionSpec as P

CX, CY, HALF, NF = 16, 128, 32, 4
HID, DEPTH = 768, 4
FEAT = NF * HALF
PIECES = (5,)
SPLIT = sum(PIECES)
SHARED = CX - 2 * SPLIT
ROWS = 24
OWN = 5
SLOTS = HALF + 10
BLOCK = 2
SIDE = (3 * NF + 3 + 2) * HALF
LEVS = (3 * NF + 2 + 3) * CX
LEV_SIDES = 8 * (3 * NF + 2 + 3 + 1)
VM = pl.BlockSpec(memory_space=pltpu.VMEM)
SM = pl.BlockSpec(memory_space=pltpu.SMEM)
HB = pl.BlockSpec(memory_space=pltpu.HBM)
F32, BF16 = jnp.float32, jnp.bfloat16
PARAMS = pltpu.CompilerParams(vmem_limit_bytes=24 * 1024 * 1024)


def cost(us):
    return pl.CostEstimate(flops=0, transcendentals=0, bytes_accessed=int(us * 3_600_000))


def shape(rows, dtype=BF16):
    return jax.ShapeDtypeStruct((rows, CY), dtype)


def side_channels():
    return [(c, d) for c in range(NF + 1) for d in range(3)] + [(NF + 1, 0), (NF + 1, 1)]


def lev_channels():
    return [(c, d) for c in range(NF) for d in range(3)] + [(NF, 0), (NF, 1)] + [(NF + 1, d) for d in range(3)]


def near_row(odd, d):
    return jnp.where(odd == 0, CX + d, ROWS - 1 - d)


def far_row(odd, d):
    return jnp.where(odd == 0, ROWS - 1 - d, CX + d)


def views(s0, hv):
    return s0.reshape(NF * SLOTS * ROWS, CY), hv.reshape(2 * SLOTS * ROWS, CY)


def place_in(s0, hv, c, slot):
    ref, k = (s0, c) if c < NF else (hv, c - NF)
    return ref, (k * SLOTS + slot) * ROWS


def beyond(lev, d):
    return jnp.where(lev == 0, OWN + HALF + d, OWN - 1 - d)


def pack_kernel(fields, hmix, vmix, edge_flip, which, s0, hv, far, near, flips, sems):
    tile = lax.axis_index("tile")
    odd = tile % 2
    pairs = [(fields.at[c], s0.at[c, OWN : OWN + HALF, 0:CX]) for c in range(NF)]
    pairs += [(hmix, hv.at[0, OWN : OWN + HALF, 0:CX]), (vmix, hv.at[1, OWN : OWN + HALF, 0:CX])]
    pairs.append((edge_flip, flips))
    copies = [pltpu.make_async_copy(src, dst, sems.at[i]) for i, (src, dst) in enumerate(pairs)]
    for copy in copies:
        copy.start()
    for copy in copies[:-1]:
        copy.wait()
    s0, hv = views(s0, hv)
    for k, (c, d) in enumerate(side_channels()):
        ref, base = place_in(s0, hv, c, OWN)
        rows = pl.ds(k * HALF, HALF)
        far_x = jnp.where(odd == 0, d, CX - 1 - d)
        near_x = CX - 1 - far_x
        far[rows, :] = ref[pl.ds(base + far_x, HALF, stride=ROWS), :].astype(BF16)
        near[rows, :] = ref[pl.ds(base + near_x, HALF, stride=ROWS), :].astype(BF16)
    copies[-1].wait()
    east = flips[(tile + 1) % edge_flip.shape[0]]
    west = flips[tile]
    which[0] = lax.axis_index("lev")
    which[1] = odd
    which[2] = jnp.where(odd == 0, east, west)
    which[3] = jnp.where(odd == 0, west, east)


def still(ref, ghost, count):
    for f in range(count):
        ref[pl.ds(pl.multiple_of((f * SLOTS + ghost) * ROWS, 8), ROWS), :] = jnp.zeros((ROWS, CY), F32)


def put_sides(s0, hv, sides, flag, at_row, odd):
    row = lax.broadcasted_iota(jnp.int32, (CY, CY), 0)
    col = lax.broadcasted_iota(jnp.int32, (CY, CY), 1)
    turn = jnp.where(jnp.where(flag > 0, CY - 1 - row, row) == col, 1.0, 0.0).astype(BF16)
    columns = jnp.dot(sides[...], turn, preferred_element_type=F32)
    for k, (c, d) in enumerate(side_channels()):
        ref, base = place_in(s0, hv, c, OWN)
        ref[pl.ds(base + at_row(odd, d), HALF, stride=ROWS), :] = columns[k * HALF : (k + 1) * HALF]


def beside_rows(s0, hv, lev, first, count):
    for c, d in lev_channels():
        slot = jnp.where(lev == 0, OWN + HALF - 1 - d, OWN + d)
        ref, base = place_in(s0, hv, c, slot)
        yield ref[pl.ds(pl.multiple_of(base + first, 8), count), :]


def near_kernel(which, s0_in, hv_in, sides, s0, hv, up):
    lev, odd = which[0], which[1]
    s0, hv = views(s0, hv)
    ghost = jnp.where(lev == 0, OWN - 1, OWN + HALF)
    still(s0, ghost, NF)
    still(hv, ghost, 2)
    put_sides(s0, hv, sides, which[2], near_row, odd)
    for k, level in enumerate(beside_rows(s0, hv, lev, 0, CX)):
        up[pl.ds(k * CX, CX), :] = level.astype(BF16)


def far_kernel(which, s0_in, hv_in, sides, s0, hv, corners):
    lev, odd = which[0], which[1]
    s0, hv = views(s0, hv)
    put_sides(s0, hv, sides, which[3], far_row, odd)
    rows = list(beside_rows(s0, hv, lev, CX, 8))
    corners[...] = jnp.concatenate(rows + [jnp.zeros((8, CY), F32)], axis=0).astype(BF16)


def load(ref, k, slot, levels, rows=ROWS):
    at = (k * SLOTS + slot) * ROWS
    at = at if isinstance(at, int) else pl.multiple_of(at, 8)
    return ref[pl.ds(at, levels * ROWS), :].reshape(levels, ROWS, CY)[:, :rows]


def save(ref, k, slot, value):
    at = (k * SLOTS + slot) * ROWS
    at = at if isinstance(at, int) else pl.multiple_of(at, 8)
    levels = value.shape[0]
    ref[pl.ds(at, levels * ROWS), :] = value.reshape(levels * ROWS, CY)


def weigh(h, v, h_east=None, h_west=None):
    h, v = 0.5 * h, 0.5 * v
    h_east = h if h_east is None else 0.5 * h_east
    h_west = h if h_west is None else 0.5 * h_west
    pairs = v[1:] + v[:-1]
    upper, lower = pairs[1:], pairs[:-1]
    c_east = h + pltpu.roll(h_east, h.shape[1] - 1, 1)
    c_west = h + pltpu.roll(h_west, 1, 1)
    c_north = h + pltpu.roll(h, CY - 1, 2)
    c_south = h + pltpu.roll(h, 1, 2)
    centre = 1.0 - (((c_east + c_west) + (c_north + c_south)) + (upper + lower))
    return (c_east, c_west, c_north, c_south, upper, lower, centre)


def coefficients(hv, coef, at, levels):
    k = weigh(load(hv, 0, at, levels), load(hv, 1, at - 1, levels + 2))
    for n, value in enumerate(k):
        save(coef, n, at, value)
    return k


def kept(coef, at, levels, rows):
    return [load(coef, n, at, levels, rows) for n in range(7)]


def advance(column, k, rows, east=None, west=None):
    cell, centre = column[1:-1], column[1:-1, :rows]
    east = cell if east is None else east
    west = cell if west is None else west
    value = k[6] * centre
    value += k[0] * pltpu.roll(east, cell.shape[1] - 1, 1)[:, :rows]
    value += k[1] * pltpu.roll(west, 1, 1)[:, :rows]
    value += k[2] * pltpu.roll(centre, CY - 1, 2)
    value += k[3] * pltpu.roll(centre, 1, 2)
    value += k[4] * column[2:, :rows]
    value += k[5] * column[:-2, :rows]
    return value


def substep(source, k, at, levels, rows, store):
    for f in range(NF):
        store(f, at, advance(load(source, f, at - 1, levels + 2), k, rows))


def into(target):
    return lambda f, at, value: save(target, f, at, value)


def into_result(advanced):
    def store(f, at, value):
        start = (f * HALF + at - OWN) * CX
        start = start if isinstance(start, int) else pl.multiple_of(start, CX)
        advanced[pl.ds(start, value.shape[0] * CX), :] = value.reshape(value.shape[0] * CX, CY)

    return store


def dynamics_kernel(which, s0, hv, advanced, s1, s2, coef):
    s0, hv = views(s0, hv)
    lev = which[0]
    ghost = jnp.where(lev == 0, OWN - 1, OWN + HALF)
    final = into_result(advanced)

    def one(i):
        at = OWN + i * BLOCK
        substep(s0, coefficients(hv, coef, at, BLOCK), at, BLOCK, ROWS, into(s1))

    def two(i):
        at = OWN - 1 + (i - 1) * BLOCK
        substep(s1, kept(coef, at, BLOCK, ROWS), at, BLOCK, ROWS, into(s2))

    def three(i):
        at = OWN + (i - 3) * BLOCK
        substep(s2, kept(coef, at, BLOCK, CX), at, BLOCK, CX, final)

    still(s1, ghost, NF)
    last = HALF // BLOCK
    for i in range(last + 3):
        if i >= 3:
            three(i)
        if 1 <= i <= last + 1:
            two(i)
        if i < last:
            one(i)
        if i in (1, last + 1):
            still(s2, ghost, NF)


def strip_kernel(which, s0, hv, advanced_in, advanced, t1, t2, coef):
    lev, odd = which[0], which[1]
    s0, hv = views(s0, hv)
    row = lax.broadcasted_iota(jnp.int32, (8, CY), 0)
    number = jnp.where(odd == 0, row, 7 - row)
    half = pl.multiple_of(odd * 8, 8)
    ghost = jnp.where(lev == 0, OWN - 1, OWN + HALF)

    def strips(ref, k, slot, levels):
        east, west = [], []
        for i in range(levels):
            base = (k * SLOTS + slot + i) * ROWS
            inner, outer = ref[pl.ds(pl.multiple_of(base + half, 8), 8), :], ref[pl.ds(base + CX, 8), :]
            east.append(jnp.where(number >= jnp.where(odd == 0, 6, 5), outer, inner))
            west.append(jnp.where(number >= jnp.where(odd == 0, 5, 6), outer, inner))
        return jnp.stack(east), jnp.stack(west)

    def get(ref, k, slot, levels):
        return ref[pl.ds((k * SLOTS + slot) * 8, levels * 8), :].reshape(levels, 8, CY)

    def put(ref, k, slot, value):
        ref[pl.ds((k * SLOTS + slot) * 8, value.shape[0] * 8), :] = value.reshape(-1, CY)

    def blank(ref):
        for f in range(NF):
            ref[pl.ds(pl.multiple_of((f * SLOTS + ghost) * 8, 8), 8), :] = jnp.zeros((8, CY), F32)

    def result_rows(f, slot, i):
        return pl.ds(pl.multiple_of((f * HALF + slot + i - OWN) * CX + half, 8), 8)

    def one(i):
        at = OWN + i * BLOCK
        h_east, h_west = strips(hv, 0, at, BLOCK)
        k = weigh(h_east, strips(hv, 1, at - 1, BLOCK + 2)[0], h_east, h_west)
        for n, value in enumerate(k):
            put(coef, n, at, value)
        for f in range(NF):
            east, west = strips(s0, f, at - 1, BLOCK + 2)
            put(t1, f, at, advance(east, k, 8, east[1:-1], west[1:-1]))

    def two(i):
        at = OWN - 1 + (i - 1) * BLOCK
        k = [get(coef, n, at, BLOCK) for n in range(7)]
        for f in range(NF):
            put(t2, f, at, advance(get(t1, f, at - 1, BLOCK + 2), k, 8))

    def three(i):
        at = OWN + (i - 3) * BLOCK
        k = [get(coef, n, at, BLOCK) for n in range(7)]
        for f in range(NF):
            value = advance(get(t2, f, at - 1, BLOCK + 2), k, 8)
            for n in range(BLOCK):
                rows = result_rows(f, at, n)
                advanced[rows, :] = jnp.where(number < 3, value[n], advanced[rows, :])

    blank(t1)
    last = HALF // BLOCK
    for i in range(last + 3):
        if i >= 3:
            three(i)
        if 1 <= i <= last + 1:
            two(i)
        if i < last:
            one(i)
        if i in (1, last + 1):
            blank(t2)


def closing_kernel(which, s0_in, hv_in, advanced_in, from_lev, corners, s0, hv, advanced, own, other, c1, c2):
    lev = which[0]
    s0, hv = views(s0, hv)
    sides = corners[...].astype(F32)
    for k, (c, d) in enumerate(lev_channels()):
        ref, base = place_in(s0, hv, c, beyond(lev, d))
        ref[pl.ds(pl.multiple_of(base, 8), CX), :] = from_lev[pl.ds(k * CX, CX), :].astype(F32)
        ref[pl.ds(pl.multiple_of(base + CX, 8), 8), :] = sides[k * 8 : (k + 1) * 8]
    at = jnp.where(lev == 0, OWN + HALF - 5, OWN - 2)
    k = weigh(load(hv, 0, at, 7), load(hv, 1, at - 1, 9))
    final = into_result(advanced)
    for f in range(NF):
        c1[...] = advance(load(s0, f, at - 1, 9), k, ROWS).reshape(7 * ROWS, CY)
        c2[...] = advance(c1[...].reshape(7, ROWS, CY), [n[1:-1] for n in k], ROWS).reshape(5 * ROWS, CY)
        final(f, at + 2, advance(c2[...].reshape(5, ROWS, CY), [n[2:-2, :CX] for n in k], CX))
    take_piece(lev, advanced, own, other, 0)


def take_columns(advanced, first, width, target):
    for i in range(width):
        target[pl.ds(i * FEAT, FEAT), :] = advanced[pl.ds(first + i, FEAT, stride=CX), :].astype(BF16)


def piece_start(lev, k):
    return jnp.where(lev == 0, 0, SPLIT) + sum(PIECES[:k])


def take_piece(lev, advanced, own, other, k):
    take_columns(advanced, piece_start(lev, k), PIECES[k], own)
    take_columns(advanced, piece_start(1 - lev, k), PIECES[k], other)


def rest_kernel(which, advanced, batch_slots, flags, shared, *rest):
    *pieces, slots, sems = rest
    lev = which[0]
    pairs = (
        (batch_slots.at[lax.axis_index("tile"), 0:8], slots),
    )
    copies = [pltpu.make_async_copy(src, dst, sems.at[i]) for i, (src, dst) in enumerate(pairs)]
    for copy in copies:
        copy.start()
    for k in range(1, len(PIECES)):
        take_piece(lev, advanced, pieces[2 * k - 2], pieces[2 * k - 1], k)
    take_columns(advanced, 2 * SPLIT, SHARED, shared)
    for copy in copies:
        copy.wait()
    flags[0] = lev
    flags[1] = jnp.where(slots[0, 0] >= 0, 1, 0)


def silu(z):
    half = 0.5 * z
    return half + half * jnp.tanh(half)


def network(flags, own, other, w_first, b_first, w_mid, b_mid, ha, hb):
    n = own.shape[0] // FEAT
    lev = flags[0]

    def flat(ref):
        return jnp.concatenate([ref[pl.ds(i * FEAT, FEAT), :] for i in range(n)], axis=1)

    def first_rows(block):
        return [w_first[pl.ds(pl.multiple_of(f * 2 * HALF + block * HALF, HALF), HALF), :] for f in range(NF)]

    weights = jnp.concatenate(first_rows(lev) + first_rows(1 - lev), axis=0)
    inputs = jnp.concatenate([flat(own), flat(other)], axis=0)
    part = lax.dot_general(inputs, weights, (((0,), (0,)), ((), ())), preferred_element_type=F32)
    ha[...] = silu(part + b_first[...]).astype(BF16)
    source, target = ha, hb
    for k in range(DEPTH):
        part = jnp.dot(source[...], w_mid[pl.ds(k * HID, HID), :], preferred_element_type=F32)
        target[...] = silu(part + b_mid[k : k + 1, :]).astype(BF16)
        source, target = target, source
    return source[...]


def outputs(w, hidden):
    return lax.dot_general(w[...], hidden, (((1,), (1,)), ((), ())), preferred_element_type=F32)


def split_kernel(
    flags, advanced, own, other, w_first, b_first, w_mid, b_mid, wo_own, wo_other,
    out_own, out_other, result, ha, hb, sem,
):
    copy = pltpu.make_async_copy(advanced, result, sem)

    @pl.when(flags[1] > 0)
    def _():
        copy.start()
        hidden = network(flags, own, other, w_first, b_first, w_mid, b_mid, ha, hb)
        for w, out in ((wo_other, out_other), (wo_own, out_own)):
            columns = outputs(w, hidden).astype(BF16)
            for i in range(SPLIT):
                out[pl.ds(i * FEAT, FEAT), :] = columns[:, i * CY : (i + 1) * CY]
        copy.wait()

    @pl.when(flags[1] == 0)
    def _():
        copy.start()
        copy.wait()


def put_columns(wide, first, source):
    for i in range(source.shape[0] // FEAT):
        wide[pl.ds(first + i, FEAT, stride=CX), :] = source[pl.ds(i * FEAT, FEAT), :].astype(F32)


def shared_kernel(flags, own, other, w_first, b_first, w_mid, b_mid, wo_own, mine, wide, ha, hb):
    lev = flags[0]

    @pl.when(flags[1] > 0)
    def _():
        put_columns(wide, piece_start(lev, 0), mine)
        result = outputs(wo_own, network(flags, own, other, w_first, b_first, w_mid, b_mid, ha, hb))
        for i in range(SHARED):
            wide[pl.ds(2 * SPLIT + i, FEAT, stride=CX), :] = result[:, i * CY : (i + 1) * CY]


def finish_kernel(flags, wide_in, theirs, wide, tendency, narrow, sems):
    lev = flags[0]
    active = flags[1] > 0
    rows = HALF * CX

    @pl.when(active)
    def _():
        put_columns(wide, piece_start(1 - lev, 0), theirs)

    copies = []
    for f in range(NF):
        part = pl.ds(f * rows, rows)

        @pl.when(active)
        def _():
            narrow[part, :] = wide[part, :].astype(BF16)

        @pl.when(jnp.logical_not(active))
        def _():
            narrow[part, :] = jnp.zeros((rows, CY), BF16)

        copies.append(pltpu.make_async_copy(narrow.at[part], tendency.at[part], sems.at[f]))
        copies[-1].start()
    for copy in copies:
        copy.wait()


def along_lev(value):
    return lax.ppermute(value, "lev", [(0, 1), (1, 0)])


def across(value, first):
    count = lax.axis_size("tile")
    pairs = [(i, (i + 1) % count) for i in range(first, count, 2)]
    return lax.ppermute(value, "tile", sorted(pairs + [(b, a) for a, b in pairs]))


def in_hbm(value):
    return pltpu.with_memory_space_constraint(value, pltpu.HBM)


def on_device(
    fields, horizontal_mix, vertical_mix, edge_flip, batch_slots,
    w_first, bias_first, w_middle, bias_middle, w_output,
):
    def scratch(*lead):
        return pltpu.VMEM((*lead, SLOTS, ROWS, CY), F32)

    def flat(count):
        return pltpu.VMEM((count * SLOTS * ROWS, CY), F32)

    which, s0, hv, far, near = pl.pallas_call(
        pack_kernel,
        in_specs=[HB] * 4,
        out_specs=[SM] + [VM] * 4,
        out_shape=[jax.ShapeDtypeStruct((4,), jnp.int32), scratch(NF), scratch(2), shape(SIDE), shape(SIDE)],
        scratch_shapes=[pltpu.SMEM(edge_flip.shape, jnp.int32), pltpu.SemaphoreType.DMA((NF + 3,))],
        cost_estimate=cost(2.1),
        compiler_params=PARAMS,
    )(in_hbm(fields), in_hbm(horizontal_mix), in_hbm(vertical_mix), in_hbm(edge_flip))
    from_far = across(far, 1)
    from_near = across(near, 0)

    def seam(kernel, sides, s0, hv, rows):
        return pl.pallas_call(
            kernel,
            in_specs=[SM] + [VM] * 3,
            out_specs=[VM] * 3,
            out_shape=[scratch(NF), scratch(2), shape(rows)],
            input_output_aliases={1: 0, 2: 1},
            cost_estimate=cost(0.7),
            compiler_params=PARAMS,
        )(which, s0, hv, sides)

    s0, hv, up = seam(near_kernel, from_near, s0, hv, LEVS)
    from_lev = along_lev(up)
    advanced = pl.pallas_call(
        dynamics_kernel,
        in_specs=[SM, VM, VM],
        out_specs=VM,
        out_shape=pltpu.VMEM((FEAT * CX, CY), F32),
        scratch_shapes=[flat(NF), flat(NF), flat(7)],
        cost_estimate=cost(3.8),
        compiler_params=PARAMS,
    )(which, s0, hv)
    wo_own, from_far, advanced = lax.optimization_barrier((w_output.reshape(HID, FEAT).T, from_far, advanced))
    wo_other = along_lev(wo_own)
    s0, hv, corners = seam(far_kernel, from_far, s0, hv, LEV_SIDES)
    corners = along_lev(corners)
    advanced = pl.pallas_call(
        strip_kernel,
        in_specs=[SM, VM, VM, VM],
        out_specs=VM,
        out_shape=pltpu.VMEM((FEAT * CX, CY), F32),
        scratch_shapes=[pltpu.VMEM((n * SLOTS * 8, CY), F32) for n in (NF, NF, 7)],
        input_output_aliases={3: 0},
        cost_estimate=cost(1.5),
        compiler_params=PARAMS,
    )(which, s0, hv, advanced)
    _, _, advanced, own, other = pl.pallas_call(
        closing_kernel,
        in_specs=[SM] + [VM] * 5,
        out_specs=[VM] * 5,
        out_shape=[scratch(NF), scratch(2), pltpu.VMEM((FEAT * CX, CY), F32)] + [shape(PIECES[0] * FEAT)] * 2,
        scratch_shapes=[pltpu.VMEM((7 * ROWS, CY), F32), pltpu.VMEM((5 * ROWS, CY), F32)],
        input_output_aliases={1: 0, 2: 1, 3: 2},
        cost_estimate=cost(1.3),
        compiler_params=PARAMS,
    )(which, s0, hv, advanced, from_lev, corners)
    sizes = [n for n in PIECES[1:] for _ in range(2)]
    w_first_v, w_mid_v = w_first.reshape(2 * FEAT, HID), w_middle.reshape(DEPTH * HID, HID)
    flags, shared, *pieces = pl.pallas_call(
        rest_kernel,
        in_specs=[SM, VM, HB],
        out_specs=[SM] + [VM] * (1 + len(sizes)),
        out_shape=[jax.ShapeDtypeStruct((2,), jnp.int32)]
        + [shape(n * FEAT) for n in [SHARED, *sizes]],
        scratch_shapes=[pltpu.SMEM((8, batch_slots.shape[1]), jnp.int32), pltpu.SemaphoreType.DMA((3,))],
        cost_estimate=cost(3.2),
        compiler_params=PARAMS,
    )(which, advanced, in_hbm(batch_slots.transpose(0, 2, 1)))
    received = along_lev(other)
    shared_other = along_lev(shared)

    b_first = bias_first.reshape(1, HID)
    mine, sent, result = pl.pallas_call(
        split_kernel,
        in_specs=[SM] + [VM] * 9,
        out_specs=[VM, VM, HB],
        out_shape=[
            shape(SPLIT * FEAT),
            shape(SPLIT * FEAT),
            pltpu.HBM((FEAT * CX, CY), F32),
        ],
        scratch_shapes=[pltpu.VMEM((SPLIT * CY, HID), BF16)] * 2 + [pltpu.SemaphoreType.DMA],
        cost_estimate=cost(4.9),
        compiler_params=PARAMS,
    )(flags, advanced, own, received, w_first_v, b_first, w_mid_v, bias_middle, wo_own, wo_other)
    theirs = along_lev(sent)
    wide = pl.pallas_call(
        shared_kernel,
        in_specs=[SM] + [VM] * 8,
        out_specs=VM,
        out_shape=pltpu.VMEM((FEAT * CX, CY), F32),
        scratch_shapes=[pltpu.VMEM((SHARED * CY, HID), BF16)] * 2,
        cost_estimate=cost(5.6),
        compiler_params=PARAMS,
    )(flags, shared, shared_other, w_first_v, b_first, w_mid_v, bias_middle, wo_own, mine)
    _, tendency = pl.pallas_call(
        finish_kernel,
        in_specs=[SM, VM, VM],
        out_specs=[VM, HB],
        out_shape=[pltpu.VMEM((FEAT * CX, CY), F32), pltpu.HBM((FEAT * CX, CY), BF16)],
        scratch_shapes=[pltpu.VMEM((FEAT * CX, CY), BF16), pltpu.SemaphoreType.DMA((NF,))],
        input_output_aliases={1: 0},
        cost_estimate=cost(1.4),
        compiler_params=PARAMS,
    )(flags, wide, theirs)
    whole = (NF, HALF, CX, CY)
    return result.reshape(whole), tendency.reshape(whole)


def solution(mesh):
    return jax.shard_map(
        on_device,
        mesh=mesh,
        in_specs=(
            P(None, "lev", "tile", None),
            P("lev", "tile", None),
            P("lev", "tile", None),
            P(),
            P(),
            P(),
            P(),
            P(),
            P(),
            P(None, None, "lev"),
        ),
        out_specs=(P(None, "lev", "tile", None), P(None, "lev", "tile", None)),
        check_vma=False,
    )
```

```python
import jax
import jax.numpy as jnp
from jax import lax
from jax.experimental import pallas as pl
from jax.experimental.pallas import tpu as pltpu
from jax.sharding import PartitionSpec as P

CX, CY, HALF, NF = 16, 128, 32, 4
HID, DEPTH = 768, 4
FEAT = NF * HALF
PIECES = (5,)
SPLIT = sum(PIECES)
SHARED = CX - 2 * SPLIT
ROWS = 24
OWN = 5
SLOTS = HALF + 10
BLOCK = 2
SIDE = (3 * NF + 3 + 2) * HALF
LEVS = (3 * NF + 2 + 3) * CX
LEV_SIDES = 8 * (3 * NF + 2 + 3 + 1)
VM = pl.BlockSpec(memory_space=pltpu.VMEM)
SM = pl.BlockSpec(memory_space=pltpu.SMEM)
HB = pl.BlockSpec(memory_space=pltpu.HBM)
F32, BF16 = jnp.float32, jnp.bfloat16
PARAMS = pltpu.CompilerParams(vmem_limit_bytes=24 * 1024 * 1024)


def cost(us):
    return pl.CostEstimate(flops=0, transcendentals=0, bytes_accessed=int(us * 3_600_000))


def shape(rows, dtype=BF16):
    return jax.ShapeDtypeStruct((rows, CY), dtype)


def side_channels():
    return [(c, d) for c in range(NF + 1) for d in range(3)] + [(NF + 1, 0), (NF + 1, 1)]


def lev_channels():
    return [(c, d) for c in range(NF) for d in range(3)] + [(NF, 0), (NF, 1)] + [(NF + 1, d) for d in range(3)]


def near_row(odd, d):
    return jnp.where(odd == 0, CX + d, ROWS - 1 - d)


def far_row(odd, d):
    return jnp.where(odd == 0, ROWS - 1 - d, CX + d)


def views(s0, hv):
    return s0.reshape(NF * SLOTS * ROWS, CY), hv.reshape(2 * SLOTS * ROWS, CY)


def place_in(s0, hv, c, slot):
    ref, k = (s0, c) if c < NF else (hv, c - NF)
    return ref, (k * SLOTS + slot) * ROWS


def beyond(lev, d):
    return jnp.where(lev == 0, OWN + HALF + d, OWN - 1 - d)


def pack_kernel(fields, hmix, vmix, edge_flip, which, s0, hv, far, near, flips, sems):
    tile = lax.axis_index("tile")
    odd = tile % 2
    pairs = [(fields.at[c], s0.at[c, OWN : OWN + HALF, 0:CX]) for c in range(NF)]
    pairs += [(hmix, hv.at[0, OWN : OWN + HALF, 0:CX]), (vmix, hv.at[1, OWN : OWN + HALF, 0:CX])]
    pairs.append((edge_flip, flips))
    copies = [pltpu.make_async_copy(src, dst, sems.at[i]) for i, (src, dst) in enumerate(pairs)]
    for copy in copies:
        copy.start()
    for copy in copies[:-1]:
        copy.wait()
    s0, hv = views(s0, hv)
    ghost = jnp.where(lax.axis_index("lev") == 0, OWN - 1, OWN + HALF)
    still(s0, ghost, NF)
    still(hv, ghost, 2)
    for k, (c, d) in enumerate(side_channels()):
        ref, base = place_in(s0, hv, c, OWN)
        rows = pl.ds(k * HALF, HALF)
        far_x = jnp.where(odd == 0, d, CX - 1 - d)
        near_x = CX - 1 - far_x
        far[rows, :] = ref[pl.ds(base + far_x, HALF, stride=ROWS), :].astype(BF16)
        near[rows, :] = ref[pl.ds(base + near_x, HALF, stride=ROWS), :].astype(BF16)
    copies[-1].wait()
    east = flips[(tile + 1) % edge_flip.shape[0]]
    west = flips[tile]
    which[0] = lax.axis_index("lev")
    which[1] = odd
    which[2] = jnp.where(odd == 0, east, west)
    which[3] = jnp.where(odd == 0, west, east)


def still(ref, ghost, count):
    for f in range(count):
        ref[pl.ds(pl.multiple_of((f * SLOTS + ghost) * ROWS, 8), ROWS), :] = jnp.zeros((ROWS, CY), F32)


def put_sides(s0, hv, sides, flag, at_row, odd):
    row = lax.broadcasted_iota(jnp.int32, (CY, CY), 0)
    col = lax.broadcasted_iota(jnp.int32, (CY, CY), 1)
    turn = jnp.where(jnp.where(flag > 0, CY - 1 - row, row) == col, 1.0, 0.0).astype(BF16)
    columns = jnp.dot(sides[...], turn, preferred_element_type=F32)
    for k, (c, d) in enumerate(side_channels()):
        ref, base = place_in(s0, hv, c, OWN)
        ref[pl.ds(base + at_row(odd, d), HALF, stride=ROWS), :] = columns[k * HALF : (k + 1) * HALF]


def beside_rows(s0, hv, lev, first, count):
    for c, d in lev_channels():
        slot = jnp.where(lev == 0, OWN + HALF - 1 - d, OWN + d)
        ref, base = place_in(s0, hv, c, slot)
        yield ref[pl.ds(pl.multiple_of(base + first, 8), count), :]


def sides_kernel(which, s0_in, hv_in, near, far, s0, hv, corners):
    lev, odd = which[0], which[1]
    s0, hv = views(s0, hv)
    put_sides(s0, hv, near, which[2], near_row, odd)
    put_sides(s0, hv, far, which[3], far_row, odd)
    rows = list(beside_rows(s0, hv, lev, CX, 8))
    corners[...] = jnp.concatenate(rows + [jnp.zeros((8, CY), F32)], axis=0).astype(BF16)


def load(ref, k, slot, levels, rows=ROWS, height=ROWS):
    at = (k * SLOTS + slot) * height
    at = at if isinstance(at, int) else pl.multiple_of(at, 8)
    return ref[pl.ds(at, levels * height), :].reshape(levels, height, CY)[:, :rows]


def save(ref, k, slot, value):
    levels, height, _ = value.shape
    ref[pl.ds((k * SLOTS + slot) * height, levels * height), :] = value.reshape(levels * height, CY)


def shift(value, by, group):
    return pltpu.roll(value.reshape(-1, group, CY), by % group, 1).reshape(value.shape)


def weigh(h, v, group, h_east=None, h_west=None):
    h, v = 0.5 * h, 0.5 * v
    h_east = h if h_east is None else 0.5 * h_east
    h_west = h if h_west is None else 0.5 * h_west
    pairs = v[1:] + v[:-1]
    upper, lower = pairs[1:], pairs[:-1]
    c_east = h + shift(h_east, -1, group)
    c_west = h + shift(h_west, 1, group)
    c_north = h + pltpu.roll(h, CY - 1, 2)
    c_south = h + pltpu.roll(h, 1, 2)
    centre = 1.0 - (((c_east + c_west) + (c_north + c_south)) + (upper + lower))
    return (c_east, c_west, c_north, c_south, upper, lower, centre)


def advance(column, k, rows, group, east=None, west=None):
    cell, centre = column[1:-1], column[1:-1, :rows]
    east = cell if east is None else east
    west = cell if west is None else west
    value = k[6] * centre
    value += k[0] * shift(east, -1, group)[:, :rows]
    value += k[1] * shift(west, 1, group)[:, :rows]
    value += k[2] * pltpu.roll(centre, CY - 1, 2)
    value += k[3] * pltpu.roll(centre, 1, 2)
    value += k[4] * column[2:, :rows]
    value += k[5] * column[:-2, :rows]
    return value


def into_result(advanced):
    def store(f, at, value):
        start = (f * HALF + at - OWN) * CX
        start = start if isinstance(start, int) else pl.multiple_of(start, CX)
        advanced[pl.ds(start, value.shape[0] * CX), :] = value.reshape(value.shape[0] * CX, CY)

    return store


def sweep(lev, source, weights, result, t1, t2, coef, group):
    ghost = jnp.where(lev == 0, OWN - 1, OWN + HALF)
    height = CX

    def kept(at):
        return [load(coef, n, at, BLOCK, height, height) for n in range(7)]

    def one(i):
        at = OWN + i * BLOCK
        k = weights(at)
        for n, value in enumerate(k):
            save(coef, n, at, value)
        for f in range(NF):
            east, west = source(f, at - 1, BLOCK + 2)
            save(t1, f, at, advance(east, k, height, group, east[1:-1], west[1:-1]))

    def two(i):
        at = OWN - 1 + (i - 1) * BLOCK
        k = kept(at)
        for f in range(NF):
            save(t2, f, at, advance(load(t1, f, at - 1, BLOCK + 2, height, height), k, height, group))

    def three(i):
        at = OWN + (i - 3) * BLOCK
        k = kept(at)
        for f in range(NF):
            result(f, at, advance(load(t2, f, at - 1, BLOCK + 2, height, height), k, height, group))

    def blank(ref):
        for f in range(NF):
            at = pl.multiple_of((f * SLOTS + ghost) * height, 8)
            ref[pl.ds(at, height), :] = jnp.zeros((height, CY), F32)

    blank(t1)
    last = HALF // BLOCK
    for i in range(last + 3):
        if i >= 3:
            three(i)
        if 1 <= i <= last + 1:
            two(i)
        if i < last:
            one(i)
        if i in (1, last + 1):
            blank(t2)


def dynamics_kernel(which, s0, hv, advanced, up, s1, s2, coef):
    s0, hv = views(s0, hv)
    lev = which[0]
    for k, level in enumerate(beside_rows(s0, hv, lev, 0, CX)):
        up[pl.ds(k * CX, CX), :] = level.astype(BF16)

    def source(f, at, levels):
        value = load(s0, f, at, levels, CX)
        return value, value

    def weights(at):
        return weigh(load(hv, 0, at, BLOCK, CX), load(hv, 1, at - 1, BLOCK + 2, CX), CX)

    sweep(lev, source, weights, into_result(advanced), s1, s2, coef, CX)


def strip_kernel(which, s0, hv, advanced_in, advanced, t1, t2, coef):
    lev = which[0]
    s0, hv = views(s0, hv)
    row = lax.broadcasted_iota(jnp.int32, (8, CY), 0)

    def strips(ref, k, slot, levels):
        east, west = [], []
        for i in range(levels):
            base = (k * SLOTS + slot + i) * ROWS
            low, high, outer = (ref[pl.ds(base + n, 8), :] for n in (0, 8, 16))
            east.append(jnp.concatenate([jnp.where(row >= 6, outer, low), jnp.where(row <= 2, outer, high)]))
            west.append(jnp.concatenate([jnp.where(row >= 5, outer, low), jnp.where(row <= 1, outer, high)]))
        return jnp.stack(east), jnp.stack(west)

    def weights(at):
        h_east, h_west = strips(hv, 0, at, BLOCK)
        return weigh(h_east, strips(hv, 1, at - 1, BLOCK + 2)[0], 8, h_east, h_west)

    def result(f, at, value):
        for n in range(BLOCK):
            start = (f * HALF + at + n - OWN) * CX
            for half, right in ((0, row < 3), (8, row > 4)):
                rows = pl.ds(start + half, 8)
                advanced[rows, :] = jnp.where(right, value[n, half : half + 8], advanced[rows, :])

    sweep(lev, lambda *place: strips(s0, *place), weights, result, t1, t2, coef, 8)


def closing_kernel(which, s0_in, hv_in, advanced_in, from_lev, corners, s0, hv, advanced, own, other, c1, c2):
    lev = which[0]
    s0, hv = views(s0, hv)
    sides = corners[...].astype(F32)
    for k, (c, d) in enumerate(lev_channels()):
        ref, base = place_in(s0, hv, c, beyond(lev, d))
        ref[pl.ds(pl.multiple_of(base, 8), CX), :] = from_lev[pl.ds(k * CX, CX), :].astype(F32)
        ref[pl.ds(pl.multiple_of(base + CX, 8), 8), :] = sides[k * 8 : (k + 1) * 8]
    at = jnp.where(lev == 0, OWN + HALF - 5, OWN - 2)
    k = weigh(load(hv, 0, at, 7), load(hv, 1, at - 1, 9), ROWS)
    final = into_result(advanced)
    for f in range(NF):
        c1[pl.ds(f * 7 * ROWS, 7 * ROWS), :] = advance(load(s0, f, at - 1, 9), k, ROWS, ROWS).reshape(7 * ROWS, CY)
    for f in range(NF):
        column = c1[pl.ds(f * 7 * ROWS, 7 * ROWS), :].reshape(7, ROWS, CY)
        c2[pl.ds(f * 5 * ROWS, 5 * ROWS), :] = advance(column, [n[1:-1] for n in k], ROWS, ROWS).reshape(5 * ROWS, CY)
    for f in range(NF):
        column = c2[pl.ds(f * 5 * ROWS, 5 * ROWS), :].reshape(5, ROWS, CY)
        final(f, at + 2, advance(column, [n[2:-2, :CX] for n in k], CX, ROWS))
    take_piece(lev, advanced, own, other, 0)


def take_columns(advanced, first, width, target):
    for i in range(width):
        target[pl.ds(i * FEAT, FEAT), :] = advanced[pl.ds(first + i, FEAT, stride=CX), :].astype(BF16)


def piece_start(lev, k):
    return jnp.where(lev == 0, 0, SPLIT) + sum(PIECES[:k])


def take_piece(lev, advanced, own, other, k):
    take_columns(advanced, piece_start(lev, k), PIECES[k], own)
    take_columns(advanced, piece_start(1 - lev, k), PIECES[k], other)


def rest_kernel(which, advanced, batch_slots, flags, shared, *rest):
    *pieces, slots, sems = rest
    lev = which[0]
    pairs = (
        (batch_slots.at[lax.axis_index("tile"), 0:8], slots),
    )
    copies = [pltpu.make_async_copy(src, dst, sems.at[i]) for i, (src, dst) in enumerate(pairs)]
    for copy in copies:
        copy.start()
    for k in range(1, len(PIECES)):
        take_piece(lev, advanced, pieces[2 * k - 2], pieces[2 * k - 1], k)
    take_columns(advanced, 2 * SPLIT, SHARED, shared)
    for copy in copies:
        copy.wait()
    flags[0] = lev
    flags[1] = jnp.where(slots[0, 0] >= 0, 1, 0)


def silu(z):
    half = 0.5 * z
    return half + half * jnp.tanh(half)


def network(flags, own, other, w_first, b_first, w_mid, b_mid, ha, hb):
    n = own.shape[0] // FEAT
    lev = flags[0]

    def flat(ref):
        return jnp.concatenate([ref[pl.ds(i * FEAT, FEAT), :] for i in range(n)], axis=1)

    def first_rows(block):
        return [w_first[pl.ds(pl.multiple_of(f * 2 * HALF + block * HALF, HALF), HALF), :] for f in range(NF)]

    weights = jnp.concatenate(first_rows(lev) + first_rows(1 - lev), axis=0)
    inputs = jnp.concatenate([flat(own), flat(other)], axis=0)
    part = lax.dot_general(inputs, weights, (((0,), (0,)), ((), ())), preferred_element_type=F32)
    ha[...] = silu(part + b_first[...]).astype(BF16)
    source, target = ha, hb
    for k in range(DEPTH):
        part = jnp.dot(source[...], w_mid[pl.ds(k * HID, HID), :], preferred_element_type=F32)
        target[...] = silu(part + b_mid[k : k + 1, :]).astype(BF16)
        source, target = target, source
    return source[...]


def outputs(w, hidden):
    return lax.dot_general(w[...], hidden, (((1,), (1,)), ((), ())), preferred_element_type=F32)


def split_kernel(
    flags, advanced, own, other, w_first, b_first, w_mid, b_mid, wo_own, wo_other,
    out_own, out_other, result, ha, hb, sem,
):
    copy = pltpu.make_async_copy(advanced, result, sem)

    @pl.when(flags[1] > 0)
    def _():
        copy.start()
        hidden = network(flags, own, other, w_first, b_first, w_mid, b_mid, ha, hb)
        for w, out in ((wo_other, out_other), (wo_own, out_own)):
            columns = outputs(w, hidden).astype(BF16)
            for i in range(SPLIT):
                out[pl.ds(i * FEAT, FEAT), :] = columns[:, i * CY : (i + 1) * CY]
        copy.wait()

    @pl.when(flags[1] == 0)
    def _():
        copy.start()
        copy.wait()


def put_columns(wide, first, source):
    for i in range(source.shape[0] // FEAT):
        wide[pl.ds(first + i, FEAT, stride=CX), :] = source[pl.ds(i * FEAT, FEAT), :].astype(F32)


def shared_kernel(flags, own, other, w_first, b_first, w_mid, b_mid, wo_own, mine, wide, ha, hb):
    lev = flags[0]

    @pl.when(flags[1] > 0)
    def _():
        put_columns(wide, piece_start(lev, 0), mine)
        result = outputs(wo_own, network(flags, own, other, w_first, b_first, w_mid, b_mid, ha, hb))
        for i in range(SHARED):
            wide[pl.ds(2 * SPLIT + i, FEAT, stride=CX), :] = result[:, i * CY : (i + 1) * CY]


def finish_kernel(flags, wide_in, theirs, wide, tendency, narrow, sems):
    lev = flags[0]
    active = flags[1] > 0
    rows = HALF * CX

    @pl.when(active)
    def _():
        put_columns(wide, piece_start(1 - lev, 0), theirs)

    copies = []
    for f in range(NF):
        part = pl.ds(f * rows, rows)

        @pl.when(active)
        def _():
            narrow[part, :] = wide[part, :].astype(BF16)

        @pl.when(jnp.logical_not(active))
        def _():
            narrow[part, :] = jnp.zeros((rows, CY), BF16)

        copies.append(pltpu.make_async_copy(narrow.at[part], tendency.at[part], sems.at[f]))
        copies[-1].start()
    for copy in copies:
        copy.wait()


def along_lev(value):
    return lax.ppermute(value, "lev", [(0, 1), (1, 0)])


def across(value, first):
    count = lax.axis_size("tile")
    pairs = [(i, (i + 1) % count) for i in range(first, count, 2)]
    return lax.ppermute(value, "tile", sorted(pairs + [(b, a) for a, b in pairs]))


def in_hbm(value):
    return pltpu.with_memory_space_constraint(value, pltpu.HBM)


def on_device(
    fields, horizontal_mix, vertical_mix, edge_flip, batch_slots,
    w_first, bias_first, w_middle, bias_middle, w_output,
):
    def scratch(*lead):
        return pltpu.VMEM((*lead, SLOTS, ROWS, CY), F32)

    def flat(count):
        return pltpu.VMEM((count * SLOTS * CX, CY), F32)

    which, s0, hv, far, near = pl.pallas_call(
        pack_kernel,
        in_specs=[HB] * 4,
        out_specs=[SM] + [VM] * 4,
        out_shape=[jax.ShapeDtypeStruct((4,), jnp.int32), scratch(NF), scratch(2), shape(SIDE), shape(SIDE)],
        scratch_shapes=[pltpu.SMEM(edge_flip.shape, jnp.int32), pltpu.SemaphoreType.DMA((NF + 3,))],
        cost_estimate=cost(2.1),
        compiler_params=PARAMS,
    )(in_hbm(fields), in_hbm(horizontal_mix), in_hbm(vertical_mix), in_hbm(edge_flip))
    from_far = across(far, 1)
    from_near = across(near, 0)

    s0, from_near = lax.optimization_barrier((s0, from_near))
    advanced, up = pl.pallas_call(
        dynamics_kernel,
        in_specs=[SM, VM, VM],
        out_specs=[VM, VM],
        out_shape=[pltpu.VMEM((FEAT * CX, CY), F32), shape(LEVS)],
        scratch_shapes=[flat(NF), flat(NF), flat(7)],
        cost_estimate=cost(2.8),
        compiler_params=PARAMS,
    )(which, s0, hv)
    from_lev = along_lev(up)
    wo_own, from_far, advanced = lax.optimization_barrier((w_output.reshape(HID, FEAT).T, from_far, advanced))
    wo_other = along_lev(wo_own)
    s0, hv, corners = pl.pallas_call(
        sides_kernel,
        in_specs=[SM] + [VM] * 4,
        out_specs=[VM] * 3,
        out_shape=[scratch(NF), scratch(2), shape(LEV_SIDES)],
        input_output_aliases={1: 0, 2: 1},
        cost_estimate=cost(0.9),
        compiler_params=PARAMS,
    )(which, s0, hv, from_near, from_far)
    corners = along_lev(corners)
    advanced = pl.pallas_call(
        strip_kernel,
        in_specs=[SM, VM, VM, VM],
        out_specs=VM,
        out_shape=pltpu.VMEM((FEAT * CX, CY), F32),
        scratch_shapes=[flat(NF), flat(NF), flat(7)],
        input_output_aliases={3: 0},
        cost_estimate=cost(1.5),
        compiler_params=PARAMS,
    )(which, s0, hv, advanced)
    _, _, advanced, own, other = pl.pallas_call(
        closing_kernel,
        in_specs=[SM] + [VM] * 5,
        out_specs=[VM] * 5,
        out_shape=[scratch(NF), scratch(2), pltpu.VMEM((FEAT * CX, CY), F32)] + [shape(PIECES[0] * FEAT)] * 2,
        scratch_shapes=[pltpu.VMEM((NF * n * ROWS, CY), F32) for n in (7, 5)],
        input_output_aliases={1: 0, 2: 1, 3: 2},
        cost_estimate=cost(1.3),
        compiler_params=PARAMS,
    )(which, s0, hv, advanced, from_lev, corners)
    sizes = [n for n in PIECES[1:] for _ in range(2)]
    w_first_v, w_mid_v = w_first.reshape(2 * FEAT, HID), w_middle.reshape(DEPTH * HID, HID)
    flags, shared, *pieces = pl.pallas_call(
        rest_kernel,
        in_specs=[SM, VM, HB],
        out_specs=[SM] + [VM] * (1 + len(sizes)),
        out_shape=[jax.ShapeDtypeStruct((2,), jnp.int32)]
        + [shape(n * FEAT) for n in [SHARED, *sizes]],
        scratch_shapes=[pltpu.SMEM((8, batch_slots.shape[1]), jnp.int32), pltpu.SemaphoreType.DMA((3,))],
        cost_estimate=cost(3.2),
        compiler_params=PARAMS,
    )(which, advanced, in_hbm(batch_slots.transpose(0, 2, 1)))
    received = along_lev(other)
    shared_other = along_lev(shared)

    b_first = bias_first.reshape(1, HID)
    mine, sent, result = pl.pallas_call(
        split_kernel,
        in_specs=[SM] + [VM] * 9,
        out_specs=[VM, VM, HB],
        out_shape=[
            shape(SPLIT * FEAT),
            shape(SPLIT * FEAT),
            pltpu.HBM((FEAT * CX, CY), F32),
        ],
        scratch_shapes=[pltpu.VMEM((SPLIT * CY, HID), BF16)] * 2 + [pltpu.SemaphoreType.DMA],
        cost_estimate=cost(4.9),
        compiler_params=PARAMS,
    )(flags, advanced, own, received, w_first_v, b_first, w_mid_v, bias_middle, wo_own, wo_other)
    theirs = along_lev(sent)
    wide = pl.pallas_call(
        shared_kernel,
        in_specs=[SM] + [VM] * 8,
        out_specs=VM,
        out_shape=pltpu.VMEM((FEAT * CX, CY), F32),
        scratch_shapes=[pltpu.VMEM((SHARED * CY, HID), BF16)] * 2,
        cost_estimate=cost(5.6),
        compiler_params=PARAMS,
    )(flags, shared, shared_other, w_first_v, b_first, w_mid_v, bias_middle, wo_own, mine)
    _, tendency = pl.pallas_call(
        finish_kernel,
        in_specs=[SM, VM, VM],
        out_specs=[VM, HB],
        out_shape=[pltpu.VMEM((FEAT * CX, CY), F32), pltpu.HBM((FEAT * CX, CY), BF16)],
        scratch_shapes=[pltpu.VMEM((FEAT * CX, CY), BF16), pltpu.SemaphoreType.DMA((NF,))],
        input_output_aliases={1: 0},
        cost_estimate=cost(1.4),
        compiler_params=PARAMS,
    )(flags, wide, theirs)
    whole = (NF, HALF, CX, CY)
    return result.reshape(whole), tendency.reshape(whole)


def solution(mesh):
    return jax.shard_map(
        on_device,
        mesh=mesh,
        in_specs=(
            P(None, "lev", "tile", None),
            P("lev", "tile", None),
            P("lev", "tile", None),
            P(),
            P(),
            P(),
            P(),
            P(),
            P(),
            P(None, None, "lev"),
        ),
        out_specs=(P(None, "lev", "tile", None), P(None, "lev", "tile", None)),
        check_vma=False,
    )
```

```python
import jax
import jax.numpy as jnp
from jax import lax
from jax.experimental import pallas as pl
from jax.experimental.pallas import tpu as pltpu
from jax.sharding import PartitionSpec as P

CX, CY, HALF, NF = 16, 128, 32, 4
HID, DEPTH = 768, 4
FEAT = NF * HALF
PIECES = (5,)
SPLIT = sum(PIECES)
SHARED = CX - 2 * SPLIT
ROWS = 24
OWN = 5
SLOTS = HALF + 10
BLOCK = 2
SIDE = (3 * NF + 3 + 2) * HALF
LEVS = (3 * NF + 2 + 3) * CX
LEV_SIDES = 8 * (3 * NF + 2 + 3 + 1)
VM = pl.BlockSpec(memory_space=pltpu.VMEM)
SM = pl.BlockSpec(memory_space=pltpu.SMEM)
HB = pl.BlockSpec(memory_space=pltpu.HBM)
F32, BF16 = jnp.float32, jnp.bfloat16
PARAMS = pltpu.CompilerParams(vmem_limit_bytes=24 * 1024 * 1024)


def cost(us):
    return pl.CostEstimate(flops=0, transcendentals=0, bytes_accessed=int(us * 3_600_000))


def shape(rows, dtype=BF16):
    return jax.ShapeDtypeStruct((rows, CY), dtype)


def side_channels():
    return [(c, d) for c in range(NF + 1) for d in range(3)] + [(NF + 1, 0), (NF + 1, 1)]


def lev_channels():
    return [(c, d) for c in range(NF) for d in range(3)] + [(NF, 0), (NF, 1)] + [(NF + 1, d) for d in range(3)]


def near_row(odd, d):
    return jnp.where(odd == 0, CX + d, ROWS - 1 - d)


def far_row(odd, d):
    return jnp.where(odd == 0, ROWS - 1 - d, CX + d)


def views(s0, hv):
    return s0.reshape(NF * SLOTS * ROWS, CY), hv.reshape(2 * SLOTS * ROWS, CY)


def place_in(s0, hv, c, slot):
    ref, k = (s0, c) if c < NF else (hv, c - NF)
    return ref, (k * SLOTS + slot) * ROWS


def beyond(lev, d):
    return jnp.where(lev == 0, OWN + HALF + d, OWN - 1 - d)


def pack_kernel(fields, hmix, vmix, edge_flip, which, s0, hv, far, near, flips, sems):
    tile = lax.axis_index("tile")
    odd = tile % 2
    pairs = [(fields.at[c], s0.at[c, OWN : OWN + HALF, 0:CX]) for c in range(NF)]
    pairs += [(hmix, hv.at[0, OWN : OWN + HALF, 0:CX]), (vmix, hv.at[1, OWN : OWN + HALF, 0:CX])]
    pairs.append((edge_flip, flips))
    copies = [pltpu.make_async_copy(src, dst, sems.at[i]) for i, (src, dst) in enumerate(pairs)]
    for copy in copies:
        copy.start()
    for copy in copies[:-1]:
        copy.wait()
    s0, hv = views(s0, hv)
    ghost = jnp.where(lax.axis_index("lev") == 0, OWN - 1, OWN + HALF)
    still(s0, ghost, NF)
    still(hv, ghost, 2)
    for k, (c, d) in enumerate(side_channels()):
        ref, base = place_in(s0, hv, c, OWN)
        rows = pl.ds(k * HALF, HALF)
        far_x = jnp.where(odd == 0, d, CX - 1 - d)
        near_x = CX - 1 - far_x
        far[rows, :] = ref[pl.ds(base + far_x, HALF, stride=ROWS), :].astype(BF16)
        near[rows, :] = ref[pl.ds(base + near_x, HALF, stride=ROWS), :].astype(BF16)
    copies[-1].wait()
    east = flips[(tile + 1) % edge_flip.shape[0]]
    west = flips[tile]
    which[0] = lax.axis_index("lev")
    which[1] = odd
    which[2] = jnp.where(odd == 0, east, west)
    which[3] = jnp.where(odd == 0, west, east)


def still(ref, ghost, count):
    for f in range(count):
        ref[pl.ds(pl.multiple_of((f * SLOTS + ghost) * ROWS, 8), ROWS), :] = jnp.zeros((ROWS, CY), F32)


def put_sides(s0, hv, sides, flag, at_row, odd):
    row = lax.broadcasted_iota(jnp.int32, (CY, CY), 0)
    col = lax.broadcasted_iota(jnp.int32, (CY, CY), 1)
    turn = jnp.where(jnp.where(flag > 0, CY - 1 - row, row) == col, 1.0, 0.0).astype(BF16)
    columns = jnp.dot(sides[...], turn, preferred_element_type=F32)
    for k, (c, d) in enumerate(side_channels()):
        ref, base = place_in(s0, hv, c, OWN)
        ref[pl.ds(base + at_row(odd, d), HALF, stride=ROWS), :] = columns[k * HALF : (k + 1) * HALF]


def beside_rows(s0, hv, lev, first, count):
    for c, d in lev_channels():
        slot = jnp.where(lev == 0, OWN + HALF - 1 - d, OWN + d)
        ref, base = place_in(s0, hv, c, slot)
        yield ref[pl.ds(pl.multiple_of(base + first, 8), count), :]


def sides_kernel(which, s0_in, hv_in, near, far, s0, hv, corners):
    lev, odd = which[0], which[1]
    s0, hv = views(s0, hv)
    put_sides(s0, hv, near, which[2], near_row, odd)
    put_sides(s0, hv, far, which[3], far_row, odd)
    rows = list(beside_rows(s0, hv, lev, CX, 8))
    corners[...] = jnp.concatenate(rows + [jnp.zeros((8, CY), F32)], axis=0).astype(BF16)


def load(ref, k, slot, levels, rows=ROWS, height=ROWS):
    at = (k * SLOTS + slot) * height
    at = at if isinstance(at, int) else pl.multiple_of(at, 8)
    return ref[pl.ds(at, levels * height), :].reshape(levels, height, CY)[:, :rows]


def save(ref, k, slot, value):
    levels, height, _ = value.shape
    ref[pl.ds((k * SLOTS + slot) * height, levels * height), :] = value.reshape(levels * height, CY)


def shift(value, by, group):
    return pltpu.roll(value.reshape(-1, group, CY), by % group, 1).reshape(value.shape)


def weigh(h, v, group, h_east=None, h_west=None):
    h, v = 0.5 * h, 0.5 * v
    h_east = h if h_east is None else 0.5 * h_east
    h_west = h if h_west is None else 0.5 * h_west
    pairs = v[1:] + v[:-1]
    upper, lower = pairs[1:], pairs[:-1]
    c_east = h + shift(h_east, -1, group)
    c_west = h + shift(h_west, 1, group)
    c_north = h + pltpu.roll(h, CY - 1, 2)
    c_south = h + pltpu.roll(h, 1, 2)
    centre = 1.0 - (((c_east + c_west) + (c_north + c_south)) + (upper + lower))
    return (c_east, c_west, c_north, c_south, upper, lower, centre)


def advance(column, k, rows, group, east=None, west=None):
    cell, centre = column[1:-1], column[1:-1, :rows]
    east = cell if east is None else east
    west = cell if west is None else west
    value = k[6] * centre
    value += k[0] * shift(east, -1, group)[:, :rows]
    value += k[1] * shift(west, 1, group)[:, :rows]
    value += k[2] * pltpu.roll(centre, CY - 1, 2)
    value += k[3] * pltpu.roll(centre, 1, 2)
    value += k[4] * column[2:, :rows]
    value += k[5] * column[:-2, :rows]
    return value


def into_result(advanced):
    def store(f, at, value):
        start = (f * HALF + at - OWN) * CX
        start = start if isinstance(start, int) else pl.multiple_of(start, CX)
        advanced[pl.ds(start, value.shape[0] * CX), :] = value.reshape(value.shape[0] * CX, CY)

    return store


def sweep(lev, source, weights, result, t1, t2, coef, group):
    ghost = jnp.where(lev == 0, OWN - 1, OWN + HALF)
    height = CX

    def kept(at):
        return [load(coef, n, at, BLOCK, height, height) for n in range(7)]

    def one(i):
        at = OWN + i * BLOCK
        k = weights(at)
        for n, value in enumerate(k):
            save(coef, n, at, value)
        for f in range(NF):
            east, west = source(f, at - 1, BLOCK + 2)
            save(t1, f, at, advance(east, k, height, group, east[1:-1], west[1:-1]))

    def two(i):
        at = OWN - 1 + (i - 1) * BLOCK
        k = kept(at)
        for f in range(NF):
            save(t2, f, at, advance(load(t1, f, at - 1, BLOCK + 2, height, height), k, height, group))

    def three(i):
        at = OWN + (i - 3) * BLOCK
        k = kept(at)
        for f in range(NF):
            result(f, at, advance(load(t2, f, at - 1, BLOCK + 2, height, height), k, height, group))

    def blank(ref):
        for f in range(NF):
            at = pl.multiple_of((f * SLOTS + ghost) * height, 8)
            ref[pl.ds(at, height), :] = jnp.zeros((height, CY), F32)

    blank(t1)
    last = HALF // BLOCK
    for i in range(last + 3):
        if i >= 3:
            three(i)
        if 1 <= i <= last + 1:
            two(i)
        if i < last:
            one(i)
        if i in (1, last + 1):
            blank(t2)


def dynamics_kernel(which, s0, hv, advanced, up, s1, s2, coef):
    s0, hv = views(s0, hv)
    lev = which[0]
    for k, level in enumerate(beside_rows(s0, hv, lev, 0, CX)):
        up[pl.ds(k * CX, CX), :] = level.astype(BF16)

    def source(f, at, levels):
        value = load(s0, f, at, levels, CX)
        return value, value

    def weights(at):
        return weigh(load(hv, 0, at, BLOCK, CX), load(hv, 1, at - 1, BLOCK + 2, CX), CX)

    sweep(lev, source, weights, into_result(advanced), s1, s2, coef, CX)


def strip_kernel(which, s0, hv, advanced_in, advanced, t1, t2, coef):
    lev = which[0]
    s0, hv = views(s0, hv)
    row = lax.broadcasted_iota(jnp.int32, (8, CY), 0)

    def strips(ref, k, slot, levels):
        east, west = [], []
        for i in range(levels):
            base = (k * SLOTS + slot + i) * ROWS
            low, high, outer = (ref[pl.ds(base + n, 8), :] for n in (0, 8, 16))
            east.append(jnp.concatenate([jnp.where(row >= 6, outer, low), jnp.where(row <= 2, outer, high)]))
            west.append(jnp.concatenate([jnp.where(row >= 5, outer, low), jnp.where(row <= 1, outer, high)]))
        return jnp.stack(east), jnp.stack(west)

    def weights(at):
        h_east, h_west = strips(hv, 0, at, BLOCK)
        return weigh(h_east, strips(hv, 1, at - 1, BLOCK + 2)[0], 8, h_east, h_west)

    def result(f, at, value):
        for n in range(BLOCK):
            start = (f * HALF + at + n - OWN) * CX
            for half, right in ((0, row < 3), (8, row > 4)):
                rows = pl.ds(start + half, 8)
                advanced[rows, :] = jnp.where(right, value[n, half : half + 8], advanced[rows, :])

    sweep(lev, lambda *place: strips(s0, *place), weights, result, t1, t2, coef, 8)


def closing_kernel(which, s0_in, hv_in, advanced_in, from_lev, corners, s0, hv, advanced, other, c1, c2):
    lev = which[0]
    s0, hv = views(s0, hv)
    sides = corners[...].astype(F32)
    for k, (c, d) in enumerate(lev_channels()):
        ref, base = place_in(s0, hv, c, beyond(lev, d))
        ref[pl.ds(pl.multiple_of(base, 8), CX), :] = from_lev[pl.ds(k * CX, CX), :].astype(F32)
        ref[pl.ds(pl.multiple_of(base + CX, 8), 8), :] = sides[k * 8 : (k + 1) * 8]
    at = jnp.where(lev == 0, OWN + HALF - 5, OWN - 2)
    k = weigh(load(hv, 0, at, 7), load(hv, 1, at - 1, 9), ROWS)
    final = into_result(advanced)
    for f in range(NF):
        c1[pl.ds(f * 7 * ROWS, 7 * ROWS), :] = advance(load(s0, f, at - 1, 9), k, ROWS, ROWS).reshape(7 * ROWS, CY)
    for f in range(NF):
        column = c1[pl.ds(f * 7 * ROWS, 7 * ROWS), :].reshape(7, ROWS, CY)
        c2[pl.ds(f * 5 * ROWS, 5 * ROWS), :] = advance(column, [n[1:-1] for n in k], ROWS, ROWS).reshape(5 * ROWS, CY)
    for f in range(NF):
        column = c2[pl.ds(f * 5 * ROWS, 5 * ROWS), :].reshape(5, ROWS, CY)
        final(f, at + 2, advance(column, [n[2:-2, :CX] for n in k], CX, ROWS))
    take_columns(advanced, piece_start(1 - lev, 0), PIECES[0], other)


def take_columns(advanced, first, width, target):
    for i in range(width):
        target[pl.ds(i * FEAT, FEAT), :] = advanced[pl.ds(first + i, FEAT, stride=CX), :].astype(BF16)


def piece_start(lev, k):
    return jnp.where(lev == 0, 0, SPLIT) + sum(PIECES[:k])


def rest_kernel(which, advanced, batch_slots, flags, shared, own, slots, sems):
    lev = which[0]
    pairs = (
        (batch_slots.at[lax.axis_index("tile"), 0:8], slots),
    )
    copies = [pltpu.make_async_copy(src, dst, sems.at[i]) for i, (src, dst) in enumerate(pairs)]
    for copy in copies:
        copy.start()
    take_columns(advanced, piece_start(lev, 0), PIECES[0], own)
    take_columns(advanced, 2 * SPLIT, SHARED, shared)
    for copy in copies:
        copy.wait()
    flags[0] = lev
    flags[1] = jnp.where(slots[0, 0] >= 0, 1, 0)


def silu(z):
    half = 0.5 * z
    return half + half * jnp.tanh(half)


def network(flags, own, other, w_first, b_first, w_mid, b_mid, ha, hb):
    n = own.shape[0] // FEAT
    lev = flags[0]

    def flat(ref):
        return jnp.concatenate([ref[pl.ds(i * FEAT, FEAT), :] for i in range(n)], axis=1)

    def first_rows(block):
        return [w_first[pl.ds(pl.multiple_of(f * 2 * HALF + block * HALF, HALF), HALF), :] for f in range(NF)]

    weights = jnp.concatenate(first_rows(lev) + first_rows(1 - lev), axis=0)
    inputs = jnp.concatenate([flat(own), flat(other)], axis=0)
    part = lax.dot_general(inputs, weights, (((0,), (0,)), ((), ())), preferred_element_type=F32)
    ha[...] = silu(part + b_first[...]).astype(BF16)
    source, target = ha, hb
    for k in range(DEPTH):
        part = jnp.dot(source[...], w_mid[pl.ds(k * HID, HID), :], preferred_element_type=F32)
        target[...] = silu(part + b_mid[k : k + 1, :]).astype(BF16)
        source, target = target, source
    return source[...]


def outputs(w, hidden):
    return lax.dot_general(w[...], hidden, (((1,), (1,)), ((), ())), preferred_element_type=F32)


def split_kernel(
    flags, advanced, own, other, w_first, b_first, w_mid, b_mid, wo_own, wo_other,
    out_own, out_other, result, ha, hb, sem,
):
    copy = pltpu.make_async_copy(advanced, result, sem)

    @pl.when(flags[1] > 0)
    def _():
        copy.start()
        hidden = network(flags, own, other, w_first, b_first, w_mid, b_mid, ha, hb)
        for w, out in ((wo_other, out_other), (wo_own, out_own)):
            columns = outputs(w, hidden).astype(BF16)
            for i in range(SPLIT):
                out[pl.ds(i * FEAT, FEAT), :] = columns[:, i * CY : (i + 1) * CY]
        copy.wait()

    @pl.when(flags[1] == 0)
    def _():
        copy.start()
        copy.wait()


def put_columns(wide, first, source):
    for i in range(source.shape[0] // FEAT):
        wide[pl.ds(first + i, FEAT, stride=CX), :] = source[pl.ds(i * FEAT, FEAT), :].astype(F32)


def shared_kernel(flags, own, other, w_first, b_first, w_mid, b_mid, wo_own, mine, wide, ha, hb):
    lev = flags[0]

    @pl.when(flags[1] > 0)
    def _():
        put_columns(wide, piece_start(lev, 0), mine)
        result = outputs(wo_own, network(flags, own, other, w_first, b_first, w_mid, b_mid, ha, hb))
        for i in range(SHARED):
            wide[pl.ds(2 * SPLIT + i, FEAT, stride=CX), :] = result[:, i * CY : (i + 1) * CY]


def finish_kernel(flags, wide_in, theirs, wide, tendency, narrow, sems):
    lev = flags[0]
    active = flags[1] > 0
    rows = HALF * CX

    @pl.when(active)
    def _():
        put_columns(wide, piece_start(1 - lev, 0), theirs)

    copies = []
    for f in range(NF):
        part = pl.ds(f * rows, rows)

        @pl.when(active)
        def _():
            narrow[part, :] = wide[part, :].astype(BF16)

        @pl.when(jnp.logical_not(active))
        def _():
            narrow[part, :] = jnp.zeros((rows, CY), BF16)

        copies.append(pltpu.make_async_copy(narrow.at[part], tendency.at[part], sems.at[f]))
        copies[-1].start()
    for copy in copies:
        copy.wait()


def along_lev(value):
    return lax.ppermute(value, "lev", [(0, 1), (1, 0)])


def across(value, first):
    count = lax.axis_size("tile")
    pairs = [(i, (i + 1) % count) for i in range(first, count, 2)]
    return lax.ppermute(value, "tile", sorted(pairs + [(b, a) for a, b in pairs]))


def in_hbm(value):
    return pltpu.with_memory_space_constraint(value, pltpu.HBM)


def on_device(
    fields, horizontal_mix, vertical_mix, edge_flip, batch_slots,
    w_first, bias_first, w_middle, bias_middle, w_output,
):
    def scratch(*lead):
        return pltpu.VMEM((*lead, SLOTS, ROWS, CY), F32)

    def flat(count):
        return pltpu.VMEM((count * SLOTS * CX, CY), F32)

    which, s0, hv, far, near = pl.pallas_call(
        pack_kernel,
        in_specs=[HB] * 4,
        out_specs=[SM] + [VM] * 4,
        out_shape=[jax.ShapeDtypeStruct((4,), jnp.int32), scratch(NF), scratch(2), shape(SIDE), shape(SIDE)],
        scratch_shapes=[pltpu.SMEM(edge_flip.shape, jnp.int32), pltpu.SemaphoreType.DMA((NF + 3,))],
        cost_estimate=cost(2.1),
        compiler_params=PARAMS,
    )(in_hbm(fields), in_hbm(horizontal_mix), in_hbm(vertical_mix), in_hbm(edge_flip))
    from_far = across(far, 1)
    from_near = across(near, 0)

    s0, from_near = lax.optimization_barrier((s0, from_near))
    advanced, up = pl.pallas_call(
        dynamics_kernel,
        in_specs=[SM, VM, VM],
        out_specs=[VM, VM],
        out_shape=[pltpu.VMEM((FEAT * CX, CY), F32), shape(LEVS)],
        scratch_shapes=[flat(NF), flat(NF), flat(7)],
        cost_estimate=cost(2.8),
        compiler_params=PARAMS,
    )(which, s0, hv)
    from_lev = along_lev(up)
    wo_own, from_far, advanced = lax.optimization_barrier((w_output.reshape(HID, FEAT).T, from_far, advanced))
    wo_other = along_lev(wo_own)
    s0, hv, corners = pl.pallas_call(
        sides_kernel,
        in_specs=[SM] + [VM] * 4,
        out_specs=[VM] * 3,
        out_shape=[scratch(NF), scratch(2), shape(LEV_SIDES)],
        input_output_aliases={1: 0, 2: 1},
        cost_estimate=cost(0.9),
        compiler_params=PARAMS,
    )(which, s0, hv, from_near, from_far)
    corners = along_lev(corners)
    advanced = pl.pallas_call(
        strip_kernel,
        in_specs=[SM, VM, VM, VM],
        out_specs=VM,
        out_shape=pltpu.VMEM((FEAT * CX, CY), F32),
        scratch_shapes=[flat(NF), flat(NF), flat(7)],
        input_output_aliases={3: 0},
        cost_estimate=cost(1.5),
        compiler_params=PARAMS,
    )(which, s0, hv, advanced)
    _, _, advanced, other = pl.pallas_call(
        closing_kernel,
        in_specs=[SM] + [VM] * 5,
        out_specs=[VM] * 4,
        out_shape=[scratch(NF), scratch(2), pltpu.VMEM((FEAT * CX, CY), F32), shape(PIECES[0] * FEAT)],
        scratch_shapes=[pltpu.VMEM((NF * n * ROWS, CY), F32) for n in (7, 5)],
        input_output_aliases={1: 0, 2: 1, 3: 2},
        cost_estimate=cost(1.3),
        compiler_params=PARAMS,
    )(which, s0, hv, advanced, from_lev, corners)
    w_first_v, w_mid_v = w_first.reshape(2 * FEAT, HID), w_middle.reshape(DEPTH * HID, HID)
    flags, shared, own = pl.pallas_call(
        rest_kernel,
        in_specs=[SM, VM, HB],
        out_specs=[SM, VM, VM],
        out_shape=[jax.ShapeDtypeStruct((2,), jnp.int32)]
        + [shape(SHARED * FEAT), shape(PIECES[0] * FEAT)],
        scratch_shapes=[pltpu.SMEM((8, batch_slots.shape[1]), jnp.int32), pltpu.SemaphoreType.DMA((3,))],
        cost_estimate=cost(3.2),
        compiler_params=PARAMS,
    )(which, advanced, in_hbm(batch_slots.transpose(0, 2, 1)))
    received = along_lev(other)
    shared_other = along_lev(shared)

    b_first = bias_first.reshape(1, HID)
    mine, sent, result = pl.pallas_call(
        split_kernel,
        in_specs=[SM] + [VM] * 9,
        out_specs=[VM, VM, HB],
        out_shape=[
            shape(SPLIT * FEAT),
            shape(SPLIT * FEAT),
            pltpu.HBM((FEAT * CX, CY), F32),
        ],
        scratch_shapes=[pltpu.VMEM((SPLIT * CY, HID), BF16)] * 2 + [pltpu.SemaphoreType.DMA],
        cost_estimate=cost(4.9),
        compiler_params=PARAMS,
    )(flags, advanced, own, received, w_first_v, b_first, w_mid_v, bias_middle, wo_own, wo_other)
    theirs = along_lev(sent)
    wide = pl.pallas_call(
        shared_kernel,
        in_specs=[SM] + [VM] * 8,
        out_specs=VM,
        out_shape=pltpu.VMEM((FEAT * CX, CY), F32),
        scratch_shapes=[pltpu.VMEM((SHARED * CY, HID), BF16)] * 2,
        cost_estimate=cost(5.6),
        compiler_params=PARAMS,
    )(flags, shared, shared_other, w_first_v, b_first, w_mid_v, bias_middle, wo_own, mine)
    _, tendency = pl.pallas_call(
        finish_kernel,
        in_specs=[SM, VM, VM],
        out_specs=[VM, HB],
        out_shape=[pltpu.VMEM((FEAT * CX, CY), F32), pltpu.HBM((FEAT * CX, CY), BF16)],
        scratch_shapes=[pltpu.VMEM((FEAT * CX, CY), BF16), pltpu.SemaphoreType.DMA((NF,))],
        input_output_aliases={1: 0},
        cost_estimate=cost(1.4),
        compiler_params=PARAMS,
    )(flags, wide, theirs)
    whole = (NF, HALF, CX, CY)
    return result.reshape(whole), tendency.reshape(whole)


def solution(mesh):
    return jax.shard_map(
        on_device,
        mesh=mesh,
        in_specs=(
            P(None, "lev", "tile", None),
            P("lev", "tile", None),
            P("lev", "tile", None),
            P(),
            P(),
            P(),
            P(),
            P(),
            P(),
            P(None, None, "lev"),
        ),
        out_specs=(P(None, "lev", "tile", None), P(None, "lev", "tile", None)),
        check_vma=False,
    )
```
